128 devices in a mesh: seq: 32 (over y, z, core), head: 4 (over x).
Axes of the slice: x: 4, y: 4, z: 4, core: 2. Of those that a mesh axis runs over, the one named last changes fastest.
Arguments:
- x_quant: bfloat16 [4096, 8192], P('seq', 'head'), may hold values from -6 to 6
- scale_exp: int32 [64, 4096], P('head', 'seq'), may hold values from -2 to 1
- dt_raw: bfloat16 [128, 4096], P('head', 'seq'), may hold values from -5 to 5
- dt_bias: float32 [128], P('head'), may hold values from -3 to -1
- a_log: float32 [128], P('head')
- skip_weight: float32 [128], P('head'), may hold values from 0.5 to 1.5
- b_proj: bfloat16 [4096, 128], P('seq'), may hold values from -4 to 4
- c_proj: bfloat16 [4096, 128], P('seq'), may hold values from -0.5 to 0.5
- doc_starts: int32 [32, 2], P('seq'), may hold values from 0 to 128, as said below
- grad_out: bfloat16 [4096, 8192], P('seq', 'head'), may hold values from -6 to 6
Outputs:
- grad_x: bfloat16 [4096, 8192], P('seq', 'head')
- grad_dt: float32 [128, 4096], P('head', 'seq')
- grad_bc: float32 [2, 4096, 128], P(None, 'seq')
- head_grads: float32 [2, 128], P(None, 'head')
The draws below stay inside these ranges and needn't reach their ends.
Inputs may be any that keep to these rules, and one draw needn't show every extreme that they name: `doc_starts`: each entry is the offset within its slab of 128 tokens of a token that begins a document, or 128 for an unused entry; a slab's entries are in no order and may repeat.
All inputs are finite; a program needn't handle non-finite values.
Results may differ from the reference program's by a relative error of at most 0.0024.
Values sent between devices are 32-bit elements; how exact they have to be, the bound alone decides.
No kernel may reach another device: no remote copies, remote signals or barrier semaphores. Data moves between devices by JAX's collectives and lax.ppermute only.
A program may use at most 128 MiB of HBM per device.

```python
import math
import jax
import jax.numpy as jnp
from jax import lax

HEADS = 128
HEAD_DIM = 64
STATE = 128
SPAN = 256
SLOTS = 2
TOK_DEV = 128
SLABS = 32
TOKENS = 4096


def draw_a_log(key, part):
    key = jax.random.fold_in(key, 11)
    key_kind, key_pos = jax.random.split(key)
    slow_heads = jax.random.uniform(key_kind, (HEADS,)) < 0.5
    spread = jax.random.uniform(key_pos, (HEADS,), jnp.float32)
    slow_low = math.log(1.0 / (8.0 * TOKENS))
    slow_high = math.log(2.0 / TOKENS)
    fast_high = math.log(1.0 / 30.0)
    log_rate = jnp.where(slow_heads, slow_low + spread * (slow_high - slow_low), slow_high + spread * (fast_high - slow_high))
    return (log_rate - math.log(0.17)).astype(jnp.float32)


def draw_doc_starts(key, part):
    key = jax.random.fold_in(key, 23)
    key_off, key_keep, key_pick = jax.random.split(key, 3)
    offsets = jax.random.randint(key_off, (SLABS, SLOTS), 0, TOK_DEV)
    keeping = jax.random.randint(key_keep, (SLABS, SLOTS), 0, 16) == 0
    picked = jax.random.randint(key_pick, (), 0, SLABS)
    row_ids = jnp.arange(SLABS, dtype=jnp.int32)[:, None]
    col_ids = jnp.arange(SLOTS, dtype=jnp.int32)[None, :]
    values = jnp.where(keeping, offsets, TOK_DEV)
    values = jnp.where((row_ids == picked) & (col_ids == 0), 0, values)
    values = jnp.where((row_ids == (picked + 1) % SLABS) & (col_ids == SLOTS - 1), TOK_DEV, values)
    return values.astype(jnp.int32)


def plant(drawn, stream_key, low, largest):
    place = [jax.random.randint(jax.random.fold_in(stream_key, axis), (), 0, length) for axis, length in enumerate(drawn.shape)]
    main_axis = drawn.shape.index(max(drawn.shape))
    next_to = place[:main_axis] + [(place[main_axis] + 1) % drawn.shape[main_axis]] + place[main_axis + 1:]
    return drawn.at[tuple(place)].set(low).at[tuple(next_to)].set(largest)


def levels(key, extent, cuts, low, top_value):
    factor_of = 1.0
    for dim, shards_of in cuts:
        steps = jax.random.uniform(jax.random.fold_in(jax.random.fold_in(key, 6), dim), (shards_of,), jnp.float32, low / len(cuts), top_value / len(cuts))
        factor_of = factor_of * jnp.repeat(jnp.exp(steps), extent[dim] // shards_of).reshape((-1,) + (1,) * (len(extent) - 1 - dim))
    return factor_of


def normal_values(key, extent, width, reach, shards=(), held_as=jnp.bfloat16):
    factor_of = levels(key, extent, shards, -0.22, 0.18) if shards else 1.0
    values = jax.random.normal(key, extent, jnp.float32) * width * factor_of
    return jnp.minimum(jnp.maximum(values, -reach), reach).astype(held_as)


def setup_inputs(seed: int = 0) -> dict:
    seeds = jax.random.split(jax.random.key(seed), 11)
    x_quant = normal_values(seeds[0], (TOKENS, HEADS * HEAD_DIM), 1.0, 6.0, ((0, 32), (1, 4)))
    scale_exp = plant(jax.random.randint(seeds[1], (HEADS * HEAD_DIM // 128, TOKENS), -2, 2), jax.random.fold_in(seeds[1], 1), -2, 1).astype(jnp.int32)
    dt_raw = normal_values(seeds[2], (HEADS, TOKENS), 1.0, 5.0, ((0, 4), (1, 32)))
    dt_bias = jnp.clip(-3.0 + 2.0 * jax.random.uniform(seeds[3], (HEADS,), jnp.float32) ** levels(seeds[3], (HEADS,), ((0, 4),), -0.2, 0.2), -3.0, -1.0)
    a_log = draw_a_log(jax.random.fold_in(seeds[10], 71), 0)
    skip_weight = jnp.clip(0.5 + 1.0 * jax.random.uniform(seeds[5], (HEADS,), jnp.float32) ** levels(seeds[5], (HEADS,), ((0, 4),), -0.2, 0.2), 0.5, 1.5)
    b_proj = normal_values(seeds[6], (TOKENS, STATE), 0.25, 4.0, ((0, 32),))
    c_proj = normal_values(seeds[7], (TOKENS, STATE), STATE ** -0.5, 0.5, ((0, 32),))
    doc_starts = draw_doc_starts(jax.random.fold_in(seeds[10], 71), 0)
    grad_out = normal_values(seeds[9], (TOKENS, HEADS * HEAD_DIM), 1.0, 6.0, ((0, 32), (1, 4)))
    return dict(x_quant=x_quant, scale_exp=scale_exp, dt_raw=dt_raw, dt_bias=dt_bias, a_log=a_log, skip_weight=skip_weight, b_proj=b_proj, c_proj=c_proj, doc_starts=doc_starts, grad_out=grad_out)


def block_step(carry, inputs, skip_vec, block_len):
    carried, running = carry
    x_block, step_block, decay_block, b_block, c_block, reset_block, grad_block = inputs
    cumulative = jnp.cumsum(decay_block, axis=1)
    segment = jnp.cumsum(reset_block)
    index_row = jnp.arange(block_len, dtype=jnp.int32)
    same_doc = (index_row[:, None] >= index_row[None, :]) & (segment[:, None] == segment[None, :])
    log_gap = cumulative[:, :, None] - cumulative[:, None, :]
    decay_mat = jnp.exp(jnp.where(same_doc[None], log_gap, -1e+30))
    kernel = jnp.dot(c_block, b_block.T, precision=lax.Precision.HIGHEST)
    scaled_input = x_block * step_block[:, :, None]
    first_doc = (segment == 0.0).astype(cumulative.dtype)
    last_doc = (segment == segment[-1]).astype(cumulative.dtype)
    enter_decay = jnp.exp(cumulative) * first_doc
    within = jnp.einsum('hts,hsp->htp', decay_mat * kernel[None], scaled_input, precision=lax.Precision.HIGHEST)
    state_read = jnp.einsum('hpn,tn->htp', carried, c_block, precision=lax.Precision.HIGHEST)
    mixer = within + enter_decay[:, :, None] * state_read + skip_vec[:, None, None] * x_block
    running = running + jnp.sum(grad_block * mixer)
    exit_decay = jnp.exp(cumulative[:, -1:] - cumulative) * last_doc
    slab_decay = jnp.exp(cumulative[:, -1]) * first_doc[-1]
    carried = slab_decay[:, None, None] * carried + jnp.einsum('hsp,sn->hpn', exit_decay[:, :, None] * scaled_input, b_block, precision=lax.Precision.HIGHEST)
    return ((carried, running), None)

def partial_step(skip_vec, block_len):

    def stepper(carry, inputs):
        return block_step(carry, inputs, skip_vec, block_len)
    return stepper

def reference(x_quant, scale_exp, dt_raw, dt_bias, a_log, skip_weight, b_proj, c_proj, doc_starts, grad_out):
    channels = HEADS * HEAD_DIM
    factor = jnp.left_shift(jnp.int32(1), scale_exp + 8).astype(jnp.float32) / 256.0
    x_vals = (x_quant.astype(jnp.float32).reshape(TOKENS, channels // 128, 128) * factor.T[:, :, None]).reshape(TOKENS, channels).astype(jnp.bfloat16)
    position = jnp.arange(TOKENS, dtype=jnp.int32)
    offsets = position % TOK_DEV
    slab_rows = doc_starts[position // TOK_DEV]
    resets = jnp.any(slab_rows == offsets[:, None], axis=1).astype(jnp.float32)
    block_len = min(SPAN, TOK_DEV)
    pieces = TOKENS // block_len
    grad_blocks = grad_out.astype(jnp.float32).reshape(pieces, block_len, HEADS, HEAD_DIM).transpose(0, 2, 1, 3)
    reset_blocks = resets.reshape(pieces, block_len)

    def loss_of(x_float, raw, b_float, c_float, log_rate, skip_vec):
        step_size = jax.nn.softplus(raw + dt_bias[:, None])
        decay_log = -jnp.exp(log_rate)[:, None] * step_size
        x_blocks = x_float.reshape(pieces, block_len, HEADS, HEAD_DIM).transpose(0, 2, 1, 3)
        step_blocks = step_size.reshape(HEADS, pieces, block_len).transpose(1, 0, 2)
        decay_blocks = decay_log.reshape(HEADS, pieces, block_len).transpose(1, 0, 2)
        b_blocks = b_float.reshape(pieces, block_len, STATE)
        c_blocks = c_float.reshape(pieces, block_len, STATE)
        stepper = jax.checkpoint(partial_step(skip_vec, block_len))
        initial = (jnp.zeros((HEADS, HEAD_DIM, STATE), jnp.float32), jnp.zeros((), jnp.float32))
        (ending, running), unused = lax.scan(stepper, initial, (x_blocks, step_blocks, decay_blocks, b_blocks, c_blocks, reset_blocks, grad_blocks))
        return running
    gradients = jax.grad(loss_of, argnums=(0, 1, 2, 3, 4, 5))(x_vals.astype(jnp.float32), dt_raw.astype(jnp.float32), b_proj.astype(jnp.float32), c_proj.astype(jnp.float32), a_log, skip_weight)
    grad_x = gradients[0].astype(jnp.bfloat16)
    grad_dt = gradients[1]
    grad_bc = jnp.stack([gradients[2], gradients[3]])
    head_grads = jnp.stack([gradients[4], gradients[5]]) / math.sqrt(TOKENS * HEAD_DIM)
    return (grad_x, grad_dt, grad_bc, head_grads)
```

```python
import functools
import math

import jax
import jax.numpy as jnp
from jax import lax
from jax.experimental import pallas as pl
from jax.experimental.pallas import tpu as pltpu
from jax.sharding import PartitionSpec as P

F32 = jnp.float32
BF16 = jnp.bfloat16
HIGHEST = lax.Precision.HIGHEST
PARTS = 2
ROWS, CHIPS = 4, 4
TOK = 128
HEADS = 32
PAIRS = 16
PART_PAIRS = PAIRS // PARTS
CHUNK_PAIRS = PART_PAIRS // CHIPS
PART_ROWS = PART_PAIRS * TOK
CHUNK_ROWS = CHUNK_PAIRS * TOK
VMEM = pl.BlockSpec(memory_space=pltpu.VMEM)
SMEM = pl.BlockSpec(memory_space=pltpu.SMEM)
VMEM_LIMIT = 24 << 20


def nn(a, b, precision=None):
    return lax.dot_general(
        a, b, (((1,), (0,)), ((), ())), preferred_element_type=F32, precision=precision
    )


def nt(a, b, precision=None):
    return lax.dot_general(
        a, b, (((1,), (1,)), ((), ())), preferred_element_type=F32, precision=precision
    )


def halves(v):
    high = v.astype(BF16)
    return high, (v - high.astype(F32)).astype(BF16)


def iota(shape, axis):
    return lax.broadcasted_iota(jnp.int32, shape, axis)


def column(row, count):
    on = iota((count, count), 0) == iota((count, count), 1)
    return jnp.sum(jnp.where(on, jnp.broadcast_to(row, (count, count)), 0.0), axis=1, keepdims=True)


def pair_column(cols, first, lanes):
    shape = (TOK, 128)
    return jnp.where(
        lanes,
        jnp.broadcast_to(cols[:, first : first + 1], shape),
        jnp.broadcast_to(cols[:, first + 1 : first + 2], shape),
    )


def states_kernel(
    place, doc, xq, scale, dt, bias, alog, b, c, g, x_out, rows_out, cols_out, decay_out, *parts
):
    core = place[0]
    sends, keeps = parts[:PARTS], parts[PARTS:]
    doc0, doc1 = doc[0, 0], doc[0, 1]
    token = iota((HEADS, TOK), 1)
    seg = (token >= doc0).astype(jnp.int32) + (token >= doc1).astype(jnp.int32)
    seg_last = (doc0 < TOK).astype(jnp.int32) + (doc1 < TOK).astype(jnp.int32)
    pre = dt[...].astype(F32) + column(bias[...], HEADS)
    step = jnp.maximum(pre, 0.0) + jnp.log1p(jnp.exp(-jnp.abs(pre)))
    rate = jnp.exp(column(alog[...], HEADS))
    upto = (iota((TOK, TOK), 0) <= iota((TOK, TOK), 1)).astype(F32)
    total = nn(-rate * step, upto, HIGHEST)
    last = jnp.broadcast_to(total[:, TOK - 1 :], (HEADS, TOK))
    enter = jnp.where(seg == 0, jnp.exp(total), 0.0)
    leave = jnp.where(seg == seg_last, jnp.exp(last - total), 0.0)
    block = jnp.where(seg_last == 0, jnp.exp(last), 0.0)
    rows_out[0] = step
    rows_out[1] = total
    rows_out[2] = enter
    rows_out[3] = leave
    rows_out[4] = pre
    rows_out[5] = block
    cols = jnp.concatenate([enter, leave * step, total, step], 0).T
    cols_out[...] = cols
    lanes = iota((TOK, 128), 1) < 64
    pick = iota((PAIRS, HEADS), 1) - 2 * iota((PAIRS, HEADS), 0)
    decay = jnp.where(
        iota((PAIRS, 128), 1) < 64,
        nn((pick == 0).astype(F32), block, HIGHEST),
        nn((pick == 1).astype(F32), block, HIGHEST),
    )
    decay_out[...] = decay
    factor = (jnp.left_shift(jnp.int32(1), scale[...] + 8).astype(F32) / 256.0).T
    b_t = b[...].astype(F32).T.astype(BF16)
    c_t = c[...].astype(F32).T.astype(BF16)
    b_t = jnp.concatenate([b_t, b_t], 1)
    c_t = jnp.concatenate([c_t, c_t], 1)
    for j in range(0, PAIRS, 2):
        left, right = [], []
        for i in (j, j + 1):
            at = slice(128 * i, 128 * i + 128)
            x_pair = xq[:, at].astype(F32) * jnp.broadcast_to(factor[:, i : i + 1], (TOK, 128))
            x_out[:, at] = x_pair.astype(BF16)
            left.append(
                jnp.concatenate(halves(pair_column(cols, HEADS + 2 * i, lanes) * x_pair), 0)
            )
            right.append(
                jnp.concatenate(
                    halves(pair_column(cols, 2 * i, lanes) * g[:, at].astype(F32)), 0
                )
            )
        state = nn(b_t, jnp.concatenate(left, 1))
        grad = nn(c_t, jnp.concatenate(right, 1))
        part = j // PART_PAIRS
        for i in (0, 1):
            at = slice(128 * i, 128 * i + 128)
            to = slice((j + i - part * PART_PAIRS) * 128, (j + i + 1 - part * PART_PAIRS) * 128)
            sends[part][to, :] = jnp.where(core == 0, state[:, at], grad[:, at])
            keeps[part][to, :] = jnp.where(core == 0, grad[:, at], state[:, at])
    for part in range(PARTS):
        own = decay[part * PART_PAIRS : (part + 1) * PART_PAIRS]
        if PART_PAIRS < 8:
            own = jnp.concatenate([own, jnp.zeros((8 - PART_PAIRS, 128), F32)], 0)
        sends[part][PART_ROWS:, :] = own
        keeps[part][PART_ROWS:, :] = own


def chip_kernel(place, keep, recv, *outs):
    spot = place[1]
    own = keep[PART_ROWS:, :]
    both = own * recv[PART_ROWS:, :]
    for distance in range(CHIPS):
        target = (spot + distance) % CHIPS
        first = pl.multiple_of(target * CHUNK_ROWS, CHUNK_ROWS)
        decay = jnp.zeros((CHUNK_PAIRS, 128), F32)
        chip = jnp.zeros((CHUNK_PAIRS, 128), F32)
        for i in range(CHIPS):
            here = slice(i * CHUNK_PAIRS, (i + 1) * CHUNK_PAIRS)
            decay = jnp.where(target == i, own[here], decay)
            chip = jnp.where(target == i, both[here], chip)
        for p in range(CHUNK_PAIRS):
            at = pl.ds(first + p * TOK, TOK)
            outs[distance][p * TOK : (p + 1) * TOK, :] = (
                keep[at, :] + decay[p : p + 1] * recv[at, :]
            )
        outs[distance][CHUNK_ROWS:, :] = jnp.concatenate(
            [chip, jnp.zeros((8 - CHUNK_PAIRS, 128), F32)], 0
        )


def orders(place):
    spots = [(place[1] + k) % CHIPS for k in range(CHIPS)]
    return [jnp.where(place[0] == 1, s, CHIPS - 1 - s) for s in spots]


def row_kernel(place, *refs):
    chunks, out = refs[:CHIPS], refs[CHIPS]
    order = orders(place)
    decays = [chunk[CHUNK_ROWS:, :] for chunk in chunks]
    weights = []
    for k in range(CHIPS):
        weight = jnp.ones((8, 128), F32)
        for m in range(CHIPS):
            if m != k:
                weight = jnp.where(order[m] > order[k], weight * decays[m], weight)
        weights.append(weight)
    for p in range(CHUNK_PAIRS):
        at = slice(p * TOK, (p + 1) * TOK)
        out[at, :] = sum(weights[k][p : p + 1] * chunks[k][at, :] for k in range(CHIPS))
    out[CHUNK_ROWS:, :] = decays[0] * decays[1] * decays[2] * decays[3]


def entry_kernel(place, *refs):
    chunks, rows, outs = refs[:CHIPS], refs[CHIPS : 2 * CHIPS - 1], refs[2 * CHIPS - 1 :]
    order = orders(place)
    decays = [chunk[CHUNK_ROWS:, :] for chunk in chunks]
    one = rows[0][CHUNK_ROWS:, :]
    two = one * rows[1][CHUNK_ROWS:, :]
    zero = jnp.zeros((8, 128), F32)
    weights = []
    for j in range(CHIPS):
        whole = jnp.ones((8, 128), F32)
        for m in range(CHIPS):
            if m != j:
                whole = jnp.where(order[m] < order[j], whole * decays[m], whole)
        terms = []
        for k in range(CHIPS):
            if k == j:
                terms.append(None)
                continue
            weight = jnp.ones((8, 128), F32)
            for m in range(CHIPS):
                if m != j and m != k:
                    between = jnp.logical_and(order[m] > order[k], order[m] < order[j])
                    weight = jnp.where(between, weight * decays[m], weight)
            terms.append(jnp.where(order[k] < order[j], weight, zero))
        weights.append((whole, terms))
    for p in range(CHUNK_PAIRS):
        at = slice(p * TOK, (p + 1) * TOK)
        row = rows[0][at, :] + one[p : p + 1] * rows[1][at, :] + two[p : p + 1] * rows[2][at, :]
        sources = [chunk[at, :] for chunk in chunks]
        for j in range(CHIPS):
            whole, terms = weights[j]
            value = whole[p : p + 1] * row
            for k in range(CHIPS):
                if k != j:
                    value = value + terms[k][p : p + 1] * sources[k]
            outs[j][at, :] = value


def selector(heads):
    return (iota((heads, heads * 64), 1) // 64 == iota((heads, heads * 64), 0)).astype(BF16)


def per_head(values, heads):
    high, low = halves(values)
    pick = selector(heads)
    return nt(pick, high) + nt(pick, low)


def within_kernel(doc, skip, x, g, b, c, rows, cols, gx_out, sums_out, bc_out, work):
    doc0, doc1 = doc[0, 0], doc[0, 1]
    source, target = iota((TOK, TOK), 0), iota((TOK, TOK), 1)
    seg_s = (source >= doc0).astype(jnp.int32) + (source >= doc1).astype(jnp.int32)
    seg_t = (target >= doc0).astype(jnp.int32) + (target >= doc1).astype(jnp.int32)
    mask = jnp.logical_and(target >= source, seg_s == seg_t)
    lanes = iota((TOK, 128), 1) < 64
    kern = nt(b[...], c[...])
    column_values = cols[...]
    kernel_sum = jnp.zeros((TOK, TOK), F32)
    flows = []
    for j in range(PAIRS):
        at = slice(128 * j, 128 * j + 128)
        x_pair, g_pair = x[:, at], g[:, at]
        zero = jnp.zeros_like(x_pair)
        x_both = jnp.concatenate([jnp.where(lanes, x_pair, zero), jnp.where(lanes, zero, x_pair)], 0)
        g_both = jnp.concatenate([jnp.where(lanes, g_pair, zero), jnp.where(lanes, zero, g_pair)], 0)
        scores = nt(x_both, g_pair)
        high, low = [], []
        for i in (0, 1):
            h = 2 * j + i
            total_s = jnp.broadcast_to(column_values[:, 64 + h : 65 + h], (TOK, TOK))
            step_s = jnp.broadcast_to(column_values[:, 96 + h : 97 + h], (TOK, TOK))
            total_t = rows[1, h : h + 1, :]
            decay = jnp.exp(jnp.where(mask, total_t - total_s, -1e30))
            score = decay * (step_s * scores[i * TOK : (i + 1) * TOK])
            kernel_sum = kernel_sum + score
            flows.append(jnp.sum(score * kern, axis=0, keepdims=True))
            weighted = halves(decay * kern)
            high.append(weighted[0])
            low.append(weighted[1])
        inner = nn(jnp.concatenate(high, 1), g_both) + nn(jnp.concatenate(low, 1), g_both)
        x_wide, g_wide = x_pair.astype(F32), g_pair.astype(F32)
        skip_row = jnp.where(iota((1, 128), 1) < 64, skip[2 * j], skip[2 * j + 1])
        gx_out[:, at] = pair_column(column_values, 96 + 2 * j, lanes) * inner + skip_row * g_wide
        work[:TOK, at] = x_wide * inner
        work[TOK:, at] = x_wide * g_wide
    sums = per_head(work[...], HEADS)
    sums_out[0] = jnp.concatenate(flows, 0)
    sums_out[1] = sums[:, :TOK]
    sums_out[2] = sums[:, TOK:]
    high, low = halves(kernel_sum)
    bc_out[0] = nn(high, c[...]) + nn(low, c[...])
    high, low = halves(kernel_sum.T)
    bc_out[1] = nn(high, b[...]) + nn(low, b[...])


def final_kernel(part, place, x, g, b, c, rows, cols, sums, gx, alog, recv, acc, past, *refs):
    mine, theirs = refs[:CHIPS], refs[CHIPS : 2 * CHIPS]
    gx_out, dt_out, bc_out, past_out, work, near = refs[2 * CHIPS :]
    core, spot = place[0], place[1]
    heads = 2 * PART_PAIRS
    first_head = part * heads
    lanes = iota((TOK, 128), 1) < 64
    column_values = cols[...]
    for k in range(CHIPS):
        target = (spot + k) % CHIPS
        first = pl.multiple_of(target * CHUNK_ROWS, CHUNK_ROWS)
        near[0, pl.ds(first, CHUNK_ROWS), :] = mine[k][...]
        near[1, pl.ds(first, CHUNK_ROWS), :] = theirs[k][...]
    b_two = jnp.concatenate([b[...], b[...]], 1)
    c_two = jnp.concatenate([c[...], c[...]], 1)
    grad_b, grad_c = acc[0], acc[1]
    for p in range(PART_PAIRS):
        j = part * PART_PAIRS + p
        at = slice(128 * j, 128 * j + 128)
        local = slice(128 * p, 128 * p + 128)
        full = recv[local, :] + recv[PART_ROWS + p : PART_ROWS + p + 1, :] * near[0, local, :]
        other = near[1, local, :]
        entry = jnp.where(core == 1, full, other)
        leave = jnp.where(core == 1, other, full)
        entry_high, entry_low = halves(entry)
        leave_high, leave_low = halves(leave)
        read = nn(c_two, jnp.concatenate([entry_high, entry_low], 0))
        back = nn(b_two, jnp.concatenate([leave_high, leave_low], 0))
        x_wide, g_wide = x[:, at].astype(F32), g[:, at].astype(F32)
        leave_step = pair_column(column_values, HEADS + 2 * j, lanes)
        gx_out[:, local] = (gx[:, at] + leave_step * back).astype(BF16)
        work[:TOK, local] = g_wide * read
        work[TOK : 2 * TOK, local] = x_wide * back
        work[2 * TOK :, local] = jnp.sum((entry * leave).reshape(TOK // 8, 8, 128), axis=0)
        high, low = halves(pair_column(column_values, 2 * j, lanes) * g_wide)
        grad_c = grad_c + nt(
            jnp.concatenate([high, low, high], 1),
            jnp.concatenate([entry_high, entry_high, entry_low], 1),
        )
        high, low = halves(leave_step * x_wide)
        grad_b = grad_b + nt(
            jnp.concatenate([high, low, high], 1),
            jnp.concatenate([leave_high, leave_high, leave_low], 1),
        )
    bc_out[0] = grad_b
    bc_out[1] = grad_c
    found = per_head(work[...], heads)
    here = slice(first_head, first_head + heads)
    step, enter, leave, pre, block = (rows[k, here, :] for k in (0, 2, 3, 4, 5))
    flow, inner_x = sums[0, here, :], sums[1, here, :]
    read_g, back_x = found[:, :TOK], found[:, TOK : 2 * TOK]
    cross = jnp.sum(found[:, 2 * TOK :], axis=1, keepdims=True)
    rate = jnp.exp(column(alog[...], HEADS))[here]
    left = leave * step * back_x
    moves = flow - step * inner_x + enter * read_g - left
    end = jnp.sum(left, axis=1, keepdims=True) + cross * block[:, :1]
    from_here = (iota((TOK, TOK), 0) >= iota((TOK, TOK), 1)).astype(F32)
    decay_grad = nn(moves, from_here, HIGHEST) + end
    step_grad = inner_x + leave * back_x - rate * decay_grad
    dt_out[...] = step_grad / (1.0 + jnp.exp(-pre))
    logs = -rate * decay_grad * step
    if part < PARTS - 1:
        past_out[...] = logs if part == 0 else jnp.concatenate([past[...], logs], 0)
    else:
        if part:
            logs = jnp.concatenate([past[...], logs], 0)
        ones = jnp.ones((8, TOK), F32)
        past_out[0] = nt(ones, logs, HIGHEST)
        past_out[1] = nt(ones, sums[2], HIGHEST)


def seq_pairs(move):
    pairs = []
    for y in range(ROWS):
        for z in range(CHIPS):
            for core in range(2):
                to = move(y, z, core)
                if to is not None:
                    pairs.append(
                        ((y * CHIPS + z) * 2 + core, (to[0] * CHIPS + to[1]) * 2 + to[2])
                    )
    return pairs


def other_core(value):
    return lax.ppermute(value, "seq", seq_pairs(lambda y, z, core: (y, z, 1 - core)))


def along_z(value, distance):
    return lax.ppermute(
        value, "seq", seq_pairs(lambda y, z, core: (y, (z + distance) % CHIPS, core))
    )


def along_y(value, distance):
    return lax.ppermute(
        value, "seq", seq_pairs(lambda y, z, core: ((y + distance) % ROWS, z, core))
    )


def onward_y(value, distance):
    def move(y, z, core):
        to = y + distance if core else y - distance
        return (to, z, core) if 0 <= to < ROWS else None

    return lax.ppermute(value, "seq", seq_pairs(move))


def call(kernel, ins, outs, name, flops=0, scratch=(), size=0):
    shapes = [jax.ShapeDtypeStruct(s, d) for s, d in outs]
    return pl.pallas_call(
        kernel,
        out_shape=shapes,
        in_specs=[SMEM if smem else VMEM for smem, _ in ins],
        out_specs=[VMEM] * len(outs),
        scratch_shapes=list(scratch),
        name=name,
        compiler_params=pltpu.CompilerParams(vmem_limit_bytes=VMEM_LIMIT),
        cost_estimate=pl.CostEstimate(flops=flops, bytes_accessed=size, transcendentals=0),
    )(*[value for _, value in ins])


def local(
    x_quant, scale_exp, dt_raw, dt_bias, a_log, skip_weight, b_proj, c_proj, doc_starts, grad_out
):
    index = lax.axis_index("seq")
    place = jnp.stack([index % 2, (index // 2) % CHIPS]).astype(jnp.int32)
    alog_row = a_log.reshape(1, HEADS)
    part_shape = (PART_ROWS + 8 * -(-PART_PAIRS // 8), 128)
    chunk_shape = (CHUNK_ROWS + 8, 128)
    made = call(
        states_kernel,
        [
            (1, place),
            (1, doc_starts),
            (0, x_quant),
            (0, scale_exp),
            (0, dt_raw),
            (0, dt_bias.reshape(1, HEADS)),
            (0, alog_row),
            (0, b_proj),
            (0, c_proj),
            (0, grad_out),
        ],
        [((TOK, 2048), BF16), ((6, HEADS, TOK), F32), ((TOK, 128), F32), ((PAIRS, 128), F32)]
        + [(part_shape, F32)] * (2 * PARTS),
        "states",
        flops=4 * 128 * 256 * 2048,
        size=4 << 20,
    )
    x_vals, rows, cols = made[:3]
    sends, keeps = made[4 : 4 + PARTS], made[4 + PARTS :]
    recvs = [other_core(s) for s in sends]
    chunks = []
    for part in range(PARTS):
        cut = call(
            chip_kernel,
            [(1, place), (0, keeps[part]), (0, recvs[part])],
            [(chunk_shape, F32)] * CHIPS,
            "chip_total",
            size=3 << 20,
        )
        chunks.append([cut[0]] + [along_z(cut[CHIPS - k], -k) for k in range(1, CHIPS)])
    gx, sums, bc = call(
        within_kernel,
        [
            (1, doc_starts),
            (1, skip_weight),
            (0, x_vals),
            (0, grad_out),
            (0, b_proj),
            (0, c_proj),
            (0, rows),
            (0, cols),
        ],
        [((TOK, 2048), F32), ((3, HEADS, TOK), F32), ((2, TOK, 128), F32)],
        "within",
        flops=2 * 32 * 3 * 128**3,
        scratch=[pltpu.VMEM((2 * TOK, 2048), F32)],
        size=4 << 20,
    )
    mine = []
    for part in range(PARTS):
        (row,) = call(
            row_kernel,
            [(1, place)] + [(0, v) for v in chunks[part]],
            [(chunk_shape, F32)],
            "row_total",
            size=1 << 20,
        )
        before = [onward_y(row, k) for k in range(1, ROWS)]
        out = call(
            entry_kernel,
            [(1, place)] + [(0, v) for v in chunks[part] + before],
            [((CHUNK_ROWS, 128), F32)] * CHIPS,
            "entries",
            size=2 << 20,
        )
        mine.append([out[0]] + [along_z(out[CHIPS - k], -k) for k in range(1, CHIPS)])
    theirs = [[other_core(v) for v in part] for part in mine]
    past = jnp.zeros((8, 128), F32)
    gx_parts, dt_parts = [], []
    for part in range(PARTS):
        last = part == PARTS - 1
        done = (part + 1) * 2 * PART_PAIRS
        gx_part, dt_part, bc, past = call(
            functools.partial(final_kernel, part),
            [(1, place)]
            + [
                (0, v)
                for v in [x_vals, grad_out, b_proj, c_proj, rows, cols, sums, gx, alog_row]
                + [recvs[part], bc, past]
                + mine[part]
                + theirs[part]
            ],
            [
                ((TOK, PART_PAIRS * 128), BF16),
                ((2 * PART_PAIRS, TOK), F32),
                ((2, TOK, 128), F32),
                ((2, 8, HEADS), F32) if last else ((done, TOK), F32),
            ],
            "final",
            flops=2 * PART_PAIRS * 128**3 * 10,
            scratch=[
                pltpu.VMEM((2 * TOK + 8, PART_PAIRS * 128), F32),
                pltpu.VMEM((2, PART_ROWS, 128), F32),
            ],
            size=4 << 20,
        )
        gx_parts.append(gx_part)
        dt_parts.append(dt_part)
    grad_x = jnp.concatenate(gx_parts, 1)
    grad_dt = jnp.concatenate(dt_parts, 0)
    grad_bc = bc
    for k in range(1, 4):
        grad_bc = grad_bc + lax.ppermute(bc, "head", [(i, (i + k) % 4) for i in range(4)])
    totals = past
    totals = totals + other_core(totals)
    totals = totals + along_z(totals, 1) + along_z(totals, 2) + along_z(totals, 3)
    totals = totals + along_y(totals, 1) + along_y(totals, 2) + along_y(totals, 3)
    head_grads = totals[:, 0, :] / math.sqrt(TOK * 32 * 64)
    return (grad_x, grad_dt, grad_bc, head_grads)


def solution(mesh):
    in_specs = (
        P("seq", "head"),
        P("head", "seq"),
        P("head", "seq"),
        P("head"),
        P("head"),
        P("head"),
        P("seq", None),
        P("seq", None),
        P("seq", None),
        P("seq", "head"),
    )
    out_specs = (P("seq", "head"), P("head", "seq"), P(None, "seq", None), P(None, "head"))
    return jax.shard_map(local, mesh=mesh, in_specs=in_specs, out_specs=out_specs, check_vma=False)
```

```python
import functools
import math

import jax
import jax.numpy as jnp
from jax import lax
from jax.experimental import pallas as pl
from jax.experimental.pallas import tpu as pltpu
from jax.sharding import PartitionSpec as P

F32 = jnp.float32
BF16 = jnp.bfloat16
HIGHEST = lax.Precision.HIGHEST
PARTS = 2
ROWS, CHIPS = 4, 4
TOK = 128
HEADS = 32
PAIRS = 16
PART_PAIRS = PAIRS // PARTS
CHUNK_PAIRS = PART_PAIRS // CHIPS
PART_ROWS = PART_PAIRS * TOK
CHUNK_ROWS = CHUNK_PAIRS * TOK
VMEM = pl.BlockSpec(memory_space=pltpu.VMEM)
SMEM = pl.BlockSpec(memory_space=pltpu.SMEM)
ANY = pl.BlockSpec(memory_space=pl.ANY)
SPACES = (VMEM, SMEM, ANY)
VMEM_LIMIT = 24 << 20


def nn(a, b, precision=None):
    return lax.dot_general(
        a, b, (((1,), (0,)), ((), ())), preferred_element_type=F32, precision=precision
    )


def nt(a, b, precision=None):
    return lax.dot_general(
        a, b, (((1,), (1,)), ((), ())), preferred_element_type=F32, precision=precision
    )


def halves(v):
    high = v.astype(BF16)
    return high, (v - high.astype(F32)).astype(BF16)


def iota(shape, axis):
    return lax.broadcasted_iota(jnp.int32, shape, axis)


def column(row, count):
    on = iota((count, count), 0) == iota((count, count), 1)
    return jnp.sum(jnp.where(on, jnp.broadcast_to(row, (count, count)), 0.0), axis=1, keepdims=True)


def pair_column(cols, first, lanes):
    shape = (TOK, 128)
    return jnp.where(
        lanes,
        jnp.broadcast_to(cols[:, first : first + 1], shape),
        jnp.broadcast_to(cols[:, first + 1 : first + 2], shape),
    )


def over_lanes(values):
    pick = iota((PAIRS, HEADS), 1) - 2 * iota((PAIRS, HEADS), 0)
    return jnp.where(
        iota((PAIRS, 128), 1) < 64,
        nn((pick == 0).astype(F32), values, HIGHEST),
        nn((pick == 1).astype(F32), values, HIGHEST),
    )


def states_kernel(
    place, doc, xq, scale, dt, bias, alog, b, c, g, x_out, rows_out, cols_out, kappa_out, *parts
):
    core = place[0]
    sends, keeps = parts[:PARTS], parts[PARTS:]
    doc0, doc1 = doc[0, 0], doc[0, 1]
    token = iota((HEADS, TOK), 1)
    seg = (token >= doc0).astype(jnp.int32) + (token >= doc1).astype(jnp.int32)
    seg_last = (doc0 < TOK).astype(jnp.int32) + (doc1 < TOK).astype(jnp.int32)
    pre = dt[...].astype(F32) + column(bias[...], HEADS)
    step = jnp.maximum(pre, 0.0) + jnp.log1p(jnp.exp(-jnp.abs(pre)))
    rate = jnp.exp(column(alog[...], HEADS))
    upto = (iota((TOK, TOK), 0) <= iota((TOK, TOK), 1)).astype(F32)
    total = nn(-rate * step, upto, HIGHEST)
    last = jnp.broadcast_to(total[:, TOK - 1 :], (HEADS, TOK))
    enter = jnp.where(seg == 0, jnp.exp(total), 0.0)
    leave = jnp.where(seg == seg_last, jnp.exp(last - total), 0.0)
    block = jnp.where(seg_last == 0, jnp.exp(last), 0.0)
    rows_out[0] = step
    rows_out[1] = total
    rows_out[2] = enter
    rows_out[3] = leave
    rows_out[4] = pre
    rows_out[5] = block
    cols = jnp.concatenate([enter, leave * step, total, step], 0).T
    cols_out[...] = cols
    decay = over_lanes(block)
    kappa_out[...] = decay * over_lanes(last)
    lanes = iota((TOK, 128), 1) < 64
    factor = (jnp.left_shift(jnp.int32(1), scale[...] + 8).astype(F32) / 256.0).T
    b_t = b[...].astype(F32).T.astype(BF16)
    c_t = c[...].astype(F32).T.astype(BF16)
    b_t = jnp.concatenate([b_t, b_t], 1)
    c_t = jnp.concatenate([c_t, c_t], 1)
    for j in range(0, PAIRS, 2):
        left, right = [], []
        for i in (j, j + 1):
            at = slice(128 * i, 128 * i + 128)
            x_pair = xq[:, at].astype(F32) * jnp.broadcast_to(factor[:, i : i + 1], (TOK, 128))
            x_out[:, at] = x_pair.astype(BF16)
            left.append(
                jnp.concatenate(halves(pair_column(cols, HEADS + 2 * i, lanes) * x_pair), 0)
            )
            right.append(
                jnp.concatenate(
                    halves(pair_column(cols, 2 * i, lanes) * g[:, at].astype(F32)), 0
                )
            )
        state = nn(b_t, jnp.concatenate(left, 1))
        grad = nn(c_t, jnp.concatenate(right, 1))
        part = j // PART_PAIRS
        for i in (0, 1):
            at = slice(128 * i, 128 * i + 128)
            to = slice((j + i - part * PART_PAIRS) * 128, (j + i + 1 - part * PART_PAIRS) * 128)
            sends[part][to, :] = jnp.where(core == 0, state[:, at], grad[:, at])
            keeps[part][to, :] = jnp.where(core == 0, grad[:, at], state[:, at])
    for part in range(PARTS):
        own = decay[part * PART_PAIRS : (part + 1) * PART_PAIRS]
        if PART_PAIRS < 8:
            own = jnp.concatenate([own, jnp.zeros((8 - PART_PAIRS, 128), F32)], 0)
        sends[part][PART_ROWS:, :] = own
        keeps[part][PART_ROWS:, :] = own


def chip_kernel(place, keep, recv, *outs):
    spot = place[1]
    own = keep[PART_ROWS:, :]
    both = own * recv[PART_ROWS:, :]
    for distance in range(CHIPS):
        target = (spot + distance) % CHIPS
        first = pl.multiple_of(target * CHUNK_ROWS, CHUNK_ROWS)
        decay = jnp.zeros((CHUNK_PAIRS, 128), F32)
        chip = jnp.zeros((CHUNK_PAIRS, 128), F32)
        for i in range(CHIPS):
            here = slice(i * CHUNK_PAIRS, (i + 1) * CHUNK_PAIRS)
            decay = jnp.where(target == i, own[here], decay)
            chip = jnp.where(target == i, both[here], chip)
        for p in range(CHUNK_PAIRS):
            at = pl.ds(first + p * TOK, TOK)
            outs[distance][p * TOK : (p + 1) * TOK, :] = (
                keep[at, :] + decay[p : p + 1] * recv[at, :]
            )
        outs[distance][CHUNK_ROWS:, :] = jnp.concatenate(
            [chip, jnp.zeros((8 - CHUNK_PAIRS, 128), F32)], 0
        )


def orders(place):
    spots = [(place[1] + k) % 4 for k in range(4)]
    return [jnp.where(place[0] == 1, s, 3 - s) for s in spots]


def product(decays, flags):
    weight = jnp.ones((8, 128), F32)
    for decay, flag in zip(decays, flags):
        weight = jnp.where(flag, weight * decay, weight)
    return weight


def path(order, decays, k, j):
    others = [m for m in range(4) if m != j and m != k]
    between = [jnp.logical_and(order[m] > order[k], order[m] < order[j]) for m in others]
    weight = product([decays[m] for m in others], between)
    return jnp.where(order[k] < order[j], weight, jnp.zeros((8, 128), F32))


def row_kernel(place, *refs):
    chunks, out = refs[:CHIPS], refs[-1]
    order = orders(place)
    decays = [chunk[CHUNK_ROWS:, :] for chunk in chunks]
    weights = []
    for k in range(CHIPS):
        others = [m for m in range(CHIPS) if m != k]
        weights.append(product([decays[m] for m in others], [order[m] > order[k] for m in others]))
    for p in range(CHUNK_PAIRS):
        at = slice(p * TOK, (p + 1) * TOK)
        out[at, :] = sum(weights[k][p : p + 1] * chunks[k][at, :] for k in range(CHIPS))
    out[CHUNK_ROWS:, :] = decays[0] * decays[1] * decays[2] * decays[3]


def entry_kernel(place, *refs):
    chunks, rows, outs = refs[:CHIPS], refs[CHIPS : 2 * CHIPS - 1], refs[2 * CHIPS :]
    one = rows[0][CHUNK_ROWS:, :]
    two = one * rows[1][CHUNK_ROWS:, :]
    order = orders(place)
    decays = [chunk[CHUNK_ROWS:, :] for chunk in chunks]
    weights = []
    for j in range(CHIPS):
        others = [m for m in range(CHIPS) if m != j]
        whole = product([decays[m] for m in others], [order[m] < order[j] for m in others])
        weights.append((whole, {k: path(order, decays, k, j) for k in others}))
    for p in range(CHUNK_PAIRS):
        at = slice(p * TOK, (p + 1) * TOK)
        row = rows[0][at, :] + one[p : p + 1] * rows[1][at, :] + two[p : p + 1] * rows[2][at, :]
        sources = [chunk[at, :] for chunk in chunks]
        for j in range(CHIPS):
            whole, terms = weights[j]
            value = whole[p : p + 1] * row
            for k, weight in terms.items():
                value = value + weight[p : p + 1] * sources[k]
            outs[j][at, :] = value


def assemble_kernel(place, *refs):
    out = refs[-1]
    for k in range(CHIPS):
        first = pl.multiple_of((place[1] + k) % CHIPS * CHUNK_ROWS, CHUNK_ROWS)
        out[pl.ds(first, CHUNK_ROWS), :] = refs[k][...]


def selector(heads):
    return (iota((heads, heads * 64), 1) // 64 == iota((heads, heads * 64), 0)).astype(BF16)


def per_head(values, heads):
    high, low = halves(values)
    pick = selector(heads)
    return nt(pick, high) + nt(pick, low)


def within_kernel(
    doc, skip, x, g, b, c, rows, cols, after, gx_out, sums_out, bc_out, u_out, w_out, heads_out, work
):
    doc0, doc1 = doc[0, 0], doc[0, 1]
    source, target = iota((TOK, TOK), 0), iota((TOK, TOK), 1)
    seg_s = (source >= doc0).astype(jnp.int32) + (source >= doc1).astype(jnp.int32)
    seg_t = (target >= doc0).astype(jnp.int32) + (target >= doc1).astype(jnp.int32)
    mask = jnp.logical_and(target >= source, seg_s == seg_t)
    lanes = iota((TOK, 128), 1) < 64
    kern = nt(b[...], c[...])
    b_t = b[...].astype(F32).T.astype(BF16)
    c_t = c[...].astype(F32).T.astype(BF16)
    b_t = jnp.concatenate([b_t, b_t], 1)
    c_t = jnp.concatenate([c_t, c_t], 1)
    columns = cols[...]
    total, step, enter, leave = (rows[k] for k in (1, 0, 2, 3))
    last = jnp.broadcast_to(total[:, TOK - 1 :], (HEADS, TOK))
    timed = jnp.concatenate(
        [enter * total, leave * step * (last - total), total, total], 0
    ).T
    kernel_sum = jnp.zeros((TOK, TOK), F32)
    flows, skips = [], []
    for j in range(PAIRS):
        at = slice(128 * j, 128 * j + 128)
        x_pair, g_pair = x[:, at], g[:, at]
        zero = jnp.zeros_like(x_pair)
        x_both = jnp.concatenate([jnp.where(lanes, x_pair, zero), jnp.where(lanes, zero, x_pair)], 0)
        g_both = jnp.concatenate([jnp.where(lanes, g_pair, zero), jnp.where(lanes, zero, g_pair)], 0)
        scores = nt(x_both, g_pair)
        high, low = [], []
        for i in (0, 1):
            h = 2 * j + i
            total_s = jnp.broadcast_to(columns[:, 64 + h : 65 + h], (TOK, TOK))
            step_s = jnp.broadcast_to(columns[:, 96 + h : 97 + h], (TOK, TOK))
            total_t = rows[1, h : h + 1, :]
            decay = jnp.exp(jnp.where(mask, total_t - total_s, -1e30))
            score = decay * (step_s * scores[i * TOK : (i + 1) * TOK])
            kernel_sum = kernel_sum + score
            flows.append(jnp.sum(score * kern, axis=0, keepdims=True))
            weighted = halves(decay * kern)
            high.append(weighted[0])
            low.append(weighted[1])
        inner = nn(jnp.concatenate(high, 1), g_both) + nn(jnp.concatenate(low, 1), g_both)
        x_wide, g_wide = x_pair.astype(F32), g_pair.astype(F32)
        skip_row = jnp.where(iota((1, 128), 1) < 64, skip[2 * j], skip[2 * j + 1])
        gx_out[:, at] = pair_column(columns, 96 + 2 * j, lanes) * inner + skip_row * g_wide
        work[:, at] = x_wide * inner
        skips.append(jnp.sum(x_wide * g_wide, axis=0, keepdims=True))
        timed_g = jnp.concatenate(halves(pair_column(timed, 2 * j, lanes) * g_wide), 0)
        timed_x = jnp.concatenate(halves(pair_column(timed, HEADS + 2 * j, lanes) * x_wide), 0)
        u_out[at, :] = nn(c_t, timed_g)
        w_out[at, :] = nn(b_t, timed_x)
    flow = jnp.concatenate(flows, 0)
    inner_x = per_head(work[...], HEADS)
    sums_out[0] = flow
    sums_out[1] = inner_x
    alone = jnp.sum((flow - step * inner_x) * total, axis=1, keepdims=True) / 64.0
    heads_out[:PAIRS, :] = over_lanes(jnp.broadcast_to(alone, (HEADS, TOK)))
    heads_out[PAIRS:, :] = jnp.concatenate(skips, 0)
    high, low = halves(kernel_sum)
    bc_out[0] = nn(high, c[...]) + nn(low, c[...])
    high, low = halves(kernel_sum.T)
    bc_out[1] = nn(high, b[...]) + nn(low, b[...])


def whole_kernel(
    part, place, recv, u, w, kappa, heads, mine, theirs, after, entry_out, leave_out, heads_out
):
    core = place[0]
    terms = []
    for p in range(PART_PAIRS):
        j = part * PART_PAIRS + p
        here = slice(128 * p, 128 * p + 128)
        at = slice(128 * j, 128 * j + 128)
        full = recv[here, :] + recv[PART_ROWS + p : PART_ROWS + p + 1, :] * mine[here, :]
        other = theirs[here, :]
        entry = jnp.where(core == 1, full, other)
        leave = jnp.where(core == 1, other, full)
        entry_out[here, :] = entry
        leave_out[here, :] = leave
        value = entry * (u[at, :] + kappa[j : j + 1, :] * leave) + w[at, :] * leave
        terms.append(jnp.sum(value, axis=0, keepdims=True))
    before = part * PART_PAIRS
    after = before + PART_PAIRS
    if before:
        heads_out[:before, :] = heads[:before, :]
    heads_out[before:after, :] = heads[before:after, :] + jnp.concatenate(terms, 0)
    heads_out[after:, :] = heads[after:, :]


def final_kernel(part, x, g, b, c, rows, cols, sums, gx, alog, acc, entry_in, leave_in, *refs):
    gx_out, dt_out, bc_out, work = refs
    heads = 2 * PART_PAIRS
    first_head = part * heads
    lanes = iota((TOK, 128), 1) < 64
    column_values = cols[...]
    b_two = jnp.concatenate([b[...], b[...]], 1)
    c_two = jnp.concatenate([c[...], c[...]], 1)
    grad_b, grad_c = acc[0], acc[1]
    for p in range(PART_PAIRS):
        j = part * PART_PAIRS + p
        at = slice(128 * j, 128 * j + 128)
        local = slice(128 * p, 128 * p + 128)
        entry, leave = entry_in[local, :], leave_in[local, :]
        entry_high, entry_low = halves(entry)
        leave_high, leave_low = halves(leave)
        read = nn(c_two, jnp.concatenate([entry_high, entry_low], 0))
        back = nn(b_two, jnp.concatenate([leave_high, leave_low], 0))
        x_wide, g_wide = x[:, at].astype(F32), g[:, at].astype(F32)
        leave_step = pair_column(column_values, HEADS + 2 * j, lanes)
        gx_out[:, local] = (gx[:, at] + leave_step * back).astype(BF16)
        work[:TOK, local] = g_wide * read
        work[TOK : 2 * TOK, local] = x_wide * back
        work[2 * TOK :, local] = jnp.sum((entry * leave).reshape(TOK // 8, 8, 128), axis=0)
        high, low = halves(pair_column(column_values, 2 * j, lanes) * g_wide)
        grad_c = grad_c + nt(
            jnp.concatenate([high, low, high], 1),
            jnp.concatenate([entry_high, entry_high, entry_low], 1),
        )
        high, low = halves(leave_step * x_wide)
        grad_b = grad_b + nt(
            jnp.concatenate([high, low, high], 1),
            jnp.concatenate([leave_high, leave_high, leave_low], 1),
        )
    bc_out[0] = grad_b
    bc_out[1] = grad_c
    found = per_head(work[...], heads)
    here = slice(first_head, first_head + heads)
    step, enter, leave, pre, block = (rows[k, here, :] for k in (0, 2, 3, 4, 5))
    flow, inner_x = sums[0, here, :], sums[1, here, :]
    read_g, back_x = found[:, :TOK], found[:, TOK : 2 * TOK]
    cross = jnp.sum(found[:, 2 * TOK :], axis=1, keepdims=True)
    rate = jnp.exp(column(alog[...], HEADS))[here]
    left = leave * step * back_x
    moves = flow - step * inner_x + enter * read_g - left
    end = jnp.sum(left, axis=1, keepdims=True) + cross * block[:, :1]
    from_here = (iota((TOK, TOK), 0) >= iota((TOK, TOK), 1)).astype(F32)
    decay_grad = nn(moves, from_here, HIGHEST) + end
    step_grad = inner_x + leave * back_x - rate * decay_grad
    dt_out[...] = step_grad / (1.0 + jnp.exp(-pre))


def heads_kernel(own, one, two, three, out):
    total = (own[...] + one[...]) + (two[...] + three[...])
    lane, head = iota((128, HEADS), 0), iota((128, HEADS), 1)
    lanes_of = (lane // 64 == head % 2).astype(F32)
    values = nn(total, lanes_of, HIGHEST)
    pair, head = iota((PAIRS, HEADS), 0), iota((PAIRS, HEADS), 1)
    on = pair == head // 2
    scale = 1.0 / math.sqrt(TOK * 32 * 64)
    for k in (0, 1):
        kept = jnp.where(on, values[k * PAIRS : (k + 1) * PAIRS], 0.0)
        out[k : k + 1, :] = jnp.sum(kept, axis=0, keepdims=True) * scale


def seq_pairs(move):
    pairs = []
    for y in range(ROWS):
        for z in range(CHIPS):
            for core in range(2):
                to = move(y, z, core)
                if to is not None:
                    pairs.append(
                        ((y * CHIPS + z) * 2 + core, (to[0] * CHIPS + to[1]) * 2 + to[2])
                    )
    return pairs


def other_core(value):
    return lax.ppermute(value, "seq", seq_pairs(lambda y, z, core: (y, z, 1 - core)))


def along_z(value, distance):
    return lax.ppermute(
        value, "seq", seq_pairs(lambda y, z, core: (y, (z + distance) % CHIPS, core))
    )


def along_y(value, distance):
    return lax.ppermute(
        value, "seq", seq_pairs(lambda y, z, core: ((y + distance) % ROWS, z, core))
    )


def onward_y(value, distance):
    def move(y, z, core):
        to = y + distance if core else y - distance
        return (to, z, core) if 0 <= to < ROWS else None

    return lax.ppermute(value, "seq", seq_pairs(move))


def call(kernel, ins, outs, name, micros, scratch=(), limit=VMEM_LIMIT):
    shapes = [jax.ShapeDtypeStruct(s, d) for s, d in outs]
    return pl.pallas_call(
        kernel,
        out_shape=shapes,
        in_specs=[SPACES[space] for space, _ in ins],
        out_specs=[VMEM] * len(outs),
        scratch_shapes=list(scratch),
        name=name,
        compiler_params=pltpu.CompilerParams(vmem_limit_bytes=limit),
        cost_estimate=pl.CostEstimate(
            flops=1 << 16, bytes_accessed=1 << 12, transcendentals=0
        ),
    )(*[value for _, value in ins])


def local(
    x_quant, scale_exp, dt_raw, dt_bias, a_log, skip_weight, b_proj, c_proj, doc_starts, grad_out
):
    index = lax.axis_index("seq")
    place = jnp.stack([index % 2, (index // 2) % CHIPS, index // (2 * CHIPS)]).astype(jnp.int32)
    alog_row = a_log.reshape(1, HEADS)
    part_shape = (PART_ROWS + 8 * -(-PART_PAIRS // 8), 128)
    chunk_shape = (CHUNK_ROWS + 8, 128)
    made = call(
        states_kernel,
        [
            (1, place),
            (1, doc_starts),
            (0, x_quant),
            (0, scale_exp),
            (0, dt_raw),
            (0, dt_bias.reshape(1, HEADS)),
            (0, alog_row),
            (0, b_proj),
            (0, c_proj),
            (0, grad_out),
        ],
        [((TOK, 2048), BF16), ((6, HEADS, TOK), F32), ((TOK, 128), F32), ((PAIRS, 128), F32)]
        + [(part_shape, F32)] * (2 * PARTS),
        "states",
        micros=3.4,
    )
    x_vals, rows, cols, kappa = made[:4]
    sends, keeps = made[4 : 4 + PARTS], made[4 + PARTS :]
    recvs = [other_core(s) for s in sends]
    chunks = []
    for part in range(PARTS):
        cut = call(
            chip_kernel,
            [(1, place), (0, keeps[part]), (0, recvs[part])],
            [(chunk_shape, F32)] * CHIPS,
            "chip_total",
            micros=0.6,
        )
        chunks.append([cut[0]] + [along_z(cut[CHIPS - k], -k) for k in range(1, CHIPS)])
    row_totals = []
    for part in range(PARTS):
        (row,) = call(
            row_kernel,
            [(1, place)] + [(0, v) for v in chunks[part]],
            [(chunk_shape, F32)],
            "row_total",
            micros=0.6,
        )
        row_totals.append(row)
    before = [[onward_y(row, k) for k in range(1, ROWS)] for row in row_totals]
    pieces = []
    for part in range(PARTS):
        out = call(
            entry_kernel,
            [(1, place)] + [(0, v) for v in chunks[part] + before[part]] + [(2, rows)],
            [((CHUNK_ROWS, 128), F32)] * CHIPS,
            "entries",
            micros=0.7,
        )
        pieces.append([out[0]] + [along_z(out[CHIPS - k], -k) for k in range(1, CHIPS)])
    gx, sums, bc, u, w, heads = call(
        within_kernel,
        [
            (1, doc_starts),
            (1, skip_weight),
            (0, x_vals),
            (0, grad_out),
            (0, b_proj),
            (0, c_proj),
            (0, rows),
            (0, cols),
            (2, pieces[-1][0]),
        ],
        [((TOK, 2048), F32), ((2, HEADS, TOK), F32), ((2, TOK, 128), F32)]
        + [((2048, 128), F32)] * 2
        + [((2 * PAIRS, 128), F32)],
        "within",
        micros=4.5,
        scratch=[pltpu.VMEM((TOK, 2048), F32)],
    )
    gx_parts, dt_parts = [], []
    for part in range(PARTS):
        (mine,) = call(
            assemble_kernel,
            [(1, place)] + [(0, v) for v in pieces[part]] + [(2, pieces[-1][0] if part == 0 else sums)],
            [((PART_ROWS, 128), F32)],
            "assemble",
            micros=0.5,
        )
        theirs = other_core(mine)
        entry, leave, heads = call(
            functools.partial(whole_kernel, part),
            [(1, place)] + [(0, v) for v in [recvs[part], u, w, kappa, heads, mine, theirs]] + [(2, bc)],
            [((PART_ROWS, 128), F32)] * 2 + [((2 * PAIRS, 128), F32)],
            "whole",
            micros=0.8,
        )
        gx_part, dt_part, bc = call(
            functools.partial(final_kernel, part),
            [
                (0, v)
                for v in [x_vals, grad_out, b_proj, c_proj, rows, cols, sums, gx]
                + [alog_row, bc, entry, leave]
            ],
            [
                ((TOK, PART_PAIRS * 128), BF16),
                ((2 * PART_PAIRS, TOK), F32),
                ((2, TOK, 128), F32),
            ],
            "final",
            micros=1.8,
            scratch=[pltpu.VMEM((2 * TOK + 8, PART_PAIRS * 128), F32)],
        )
        gx_parts.append(gx_part)
        dt_parts.append(dt_part)
    grad_x = jnp.concatenate(gx_parts, 1)
    grad_dt = jnp.concatenate(dt_parts, 0)
    grad_bc = bc
    for k in range(1, 4):
        grad_bc = grad_bc + lax.ppermute(bc, "head", [(i, (i + k) % 4) for i in range(4)])
    heads = heads + other_core(heads)
    heads = heads + along_z(heads, 1) + along_z(heads, 2) + along_z(heads, 3)
    (head_grads,) = call(
        heads_kernel,
        [(0, heads)] + [(0, along_y(heads, k)) for k in (1, 2, 3)],
        [((2, HEADS), F32)],
        "head_grads",
        micros=0.5,
    )
    return (grad_x, grad_dt, grad_bc, head_grads)


def solution(mesh):
    in_specs = (
        P("seq", "head"),
        P("head", "seq"),
        P("head", "seq"),
        P("head"),
        P("head"),
        P("head"),
        P("seq", None),
        P("seq", None),
        P("seq", None),
        P("seq", "head"),
    )
    out_specs = (P("seq", "head"), P("head", "seq"), P(None, "seq", None), P(None, "head"))
    return jax.shard_map(local, mesh=mesh, in_specs=in_specs, out_specs=out_specs, check_vma=False)
```

```python
import functools
import math

import jax
import jax.numpy as jnp
from jax import lax
from jax.experimental import pallas as pl
from jax.experimental.pallas import tpu as pltpu
from jax.sharding import PartitionSpec as P

F32 = jnp.float32
BF16 = jnp.bfloat16
HIGHEST = lax.Precision.HIGHEST
PARTS = 2
ROWS, CHIPS = 4, 4
TOK = 128
HEADS = 32
PAIRS = 16
PART_PAIRS = PAIRS // PARTS
CHUNK_PAIRS = PART_PAIRS // CHIPS
PART_ROWS = PART_PAIRS * TOK
CHUNK_ROWS = CHUNK_PAIRS * TOK
VMEM = pl.BlockSpec(memory_space=pltpu.VMEM)
SMEM = pl.BlockSpec(memory_space=pltpu.SMEM)
ORDER_ROW = (3, 1, 2, 0)
ORDER_ENTRY = (3, 0, 1, 2)
ORDER_ASSEMBLE = (1, 0, 2, 3)
ORDER_Y = (0, 2, 1)
ANY = pl.BlockSpec(memory_space=pl.ANY)
SPACES = (VMEM, SMEM, ANY)
VMEM_LIMIT = 24 << 20
COST = pl.CostEstimate(flops=1 << 16, bytes_accessed=1 << 12, transcendentals=0)


def nn(a, b, precision=None):
    return lax.dot_general(
        a, b, (((1,), (0,)), ((), ())), preferred_element_type=F32, precision=precision
    )


def nt(a, b, precision=None):
    return lax.dot_general(
        a, b, (((1,), (1,)), ((), ())), preferred_element_type=F32, precision=precision
    )


def halves(v):
    high = v.astype(BF16)
    return high, (v - high.astype(F32)).astype(BF16)


def iota(shape, axis):
    return lax.broadcasted_iota(jnp.int32, shape, axis)


def column(row, count):
    on = iota((count, count), 0) == iota((count, count), 1)
    return jnp.sum(jnp.where(on, jnp.broadcast_to(row, (count, count)), 0.0), axis=1, keepdims=True)


def pair_column(cols, first, lanes):
    shape = (TOK, 128)
    return jnp.where(
        lanes,
        jnp.broadcast_to(cols[:, first : first + 1], shape),
        jnp.broadcast_to(cols[:, first + 1 : first + 2], shape),
    )


def over_lanes(values):
    heads = values.shape[0]
    pick = iota((heads // 2, heads), 1) - 2 * iota((heads // 2, heads), 0)
    return jnp.where(
        iota((heads // 2, 128), 1) < 64,
        nn((pick == 0).astype(F32), values, HIGHEST),
        nn((pick == 1).astype(F32), values, HIGHEST),
    )


def states_kernel(
    place, doc, xq, scale, dt, bias, alog, b, c, g, x_out, rows_out, cols_out, kappa_out, *parts
):
    core = place[0]
    sends, keeps = parts[:PARTS], parts[PARTS:]
    doc0, doc1 = doc[0, 0], doc[0, 1]
    token = iota((HEADS, TOK), 1)
    seg = (token >= doc0).astype(jnp.int32) + (token >= doc1).astype(jnp.int32)
    seg_last = (doc0 < TOK).astype(jnp.int32) + (doc1 < TOK).astype(jnp.int32)
    pre = dt[...].astype(F32) + column(bias[...], HEADS)
    step = jnp.maximum(pre, 0.0) + jnp.log1p(jnp.exp(-jnp.abs(pre)))
    rate = jnp.exp(column(alog[...], HEADS))
    upto = (iota((TOK, TOK), 0) <= iota((TOK, TOK), 1)).astype(F32)
    total = nn(-rate * step, upto, HIGHEST)
    last = jnp.broadcast_to(total[:, TOK - 1 :], (HEADS, TOK))
    enter = jnp.where(seg == 0, jnp.exp(total), 0.0)
    leave = jnp.where(seg == seg_last, jnp.exp(last - total), 0.0)
    block = jnp.where(seg_last == 0, jnp.exp(last), 0.0)
    rows_out[0] = step
    rows_out[1] = total
    rows_out[2] = enter
    rows_out[3] = leave
    rows_out[4] = pre
    rows_out[5] = block
    cols = jnp.concatenate([enter, leave * step, total, step], 0).T
    cols_out[...] = cols
    decay = over_lanes(block)
    kappa_out[...] = decay * over_lanes(last)
    lanes = iota((TOK, 128), 1) < 64
    factor = (jnp.left_shift(jnp.int32(1), scale[...] + 8).astype(F32) / 256.0).T
    b_t = b[...].astype(F32).T.astype(BF16)
    c_t = c[...].astype(F32).T.astype(BF16)
    b_t = jnp.concatenate([b_t, b_t], 1)
    c_t = jnp.concatenate([c_t, c_t], 1)
    for j in range(0, PAIRS, 2):
        left, right = [], []
        for i in (j, j + 1):
            at = slice(128 * i, 128 * i + 128)
            x_pair = xq[:, at].astype(F32) * jnp.broadcast_to(factor[:, i : i + 1], (TOK, 128))
            x_out[:, at] = x_pair.astype(BF16)
            left.append(
                jnp.concatenate(halves(pair_column(cols, HEADS + 2 * i, lanes) * x_pair), 0)
            )
            right.append(
                jnp.concatenate(
                    halves(pair_column(cols, 2 * i, lanes) * g[:, at].astype(F32)), 0
                )
            )
        state = nn(b_t, jnp.concatenate(left, 1))
        grad = nn(c_t, jnp.concatenate(right, 1))
        part = j // PART_PAIRS
        for i in (0, 1):
            at = slice(128 * i, 128 * i + 128)
            to = slice((j + i - part * PART_PAIRS) * 128, (j + i + 1 - part * PART_PAIRS) * 128)
            sends[part][to, :] = jnp.where(core == 0, state[:, at], grad[:, at])
            keeps[part][to, :] = jnp.where(core == 0, grad[:, at], state[:, at])
    for part in range(PARTS):
        own = decay[part * PART_PAIRS : (part + 1) * PART_PAIRS]
        if PART_PAIRS < 8:
            own = jnp.concatenate([own, jnp.zeros((8 - PART_PAIRS, 128), F32)], 0)
        sends[part][PART_ROWS:, :] = own
        keeps[part][PART_ROWS:, :] = own


def chip_kernel(place, keep, recv, *outs):
    spot = place[1]
    own = keep[PART_ROWS:, :]
    both = own * recv[PART_ROWS:, :]
    for distance in range(CHIPS):
        target = (spot + distance) % CHIPS
        first = pl.multiple_of(target * CHUNK_ROWS, CHUNK_ROWS)
        decay = jnp.zeros((CHUNK_PAIRS, 128), F32)
        chip = jnp.zeros((CHUNK_PAIRS, 128), F32)
        for i in range(CHIPS):
            here = slice(i * CHUNK_PAIRS, (i + 1) * CHUNK_PAIRS)
            decay = jnp.where(target == i, own[here], decay)
            chip = jnp.where(target == i, both[here], chip)
        for p in range(CHUNK_PAIRS):
            at = pl.ds(first + p * TOK, TOK)
            outs[distance][p * TOK : (p + 1) * TOK, :] = (
                keep[at, :] + decay[p : p + 1] * recv[at, :]
            )
        outs[distance][CHUNK_ROWS:, :] = jnp.concatenate(
            [chip, jnp.zeros((8 - CHUNK_PAIRS, 128), F32)], 0
        )


def orders(place):
    spots = [(place[1] + k) % 4 for k in range(4)]
    return [jnp.where(place[0] == 1, s, 3 - s) for s in spots]


def product(decays, flags):
    weight = jnp.ones((8, 128), F32)
    for decay, flag in zip(decays, flags):
        weight = jnp.where(flag, weight * decay, weight)
    return weight


def path(order, decays, k, j):
    others = [m for m in range(4) if m != j and m != k]
    between = [jnp.logical_and(order[m] > order[k], order[m] < order[j]) for m in others]
    weight = product([decays[m] for m in others], between)
    return jnp.where(order[k] < order[j], weight, jnp.zeros((8, 128), F32))


def row_kernel(place, *refs):
    chunks, out = [refs[ORDER_ROW.index(k)] for k in range(CHIPS)], refs[-1]
    order = orders(place)
    decays = [chunk[CHUNK_ROWS:, :] for chunk in chunks]
    weights = []
    for k in range(CHIPS):
        others = [m for m in range(CHIPS) if m != k]
        weights.append(product([decays[m] for m in others], [order[m] > order[k] for m in others]))
    for p in range(CHUNK_PAIRS):
        at = slice(p * TOK, (p + 1) * TOK)
        out[at, :] = sum(weights[k][p : p + 1] * chunks[k][at, :] for k in range(CHIPS))
    out[CHUNK_ROWS:, :] = decays[0] * decays[1] * decays[2] * decays[3]


def entry_kernel(place, *refs):
    rows = [refs[ORDER_Y.index(k)] for k in range(ROWS - 1)]
    chunks = [refs[ROWS - 1 + ORDER_ENTRY.index(k)] for k in range(CHIPS)]
    outs = refs[2 * CHIPS :]
    one = rows[0][CHUNK_ROWS:, :]
    two = one * rows[1][CHUNK_ROWS:, :]
    order = orders(place)
    decays = [chunk[CHUNK_ROWS:, :] for chunk in chunks]
    weights = []
    for j in range(CHIPS):
        others = [m for m in range(CHIPS) if m != j]
        whole = product([decays[m] for m in others], [order[m] < order[j] for m in others])
        weights.append((whole, {k: path(order, decays, k, j) for k in others}))
    for p in range(CHUNK_PAIRS):
        at = slice(p * TOK, (p + 1) * TOK)
        row = rows[0][at, :] + one[p : p + 1] * rows[1][at, :] + two[p : p + 1] * rows[2][at, :]
        sources = [chunk[at, :] for chunk in chunks]
        for j in range(CHIPS):
            whole, terms = weights[j]
            value = whole[p : p + 1] * row
            for k, weight in terms.items():
                value = value + weight[p : p + 1] * sources[k]
            outs[j][at, :] = value


def assemble_kernel(place, *refs):
    out = refs[-1]
    for k in range(CHIPS):
        first = pl.multiple_of((place[1] + k) % CHIPS * CHUNK_ROWS, CHUNK_ROWS)
        out[pl.ds(first, CHUNK_ROWS), :] = refs[ORDER_ASSEMBLE.index(k)][...]


def selector(heads):
    return (iota((heads, heads * 64), 1) // 64 == iota((heads, heads * 64), 0)).astype(BF16)


def per_head(values, heads):
    high, low = halves(values)
    pick = selector(heads)
    return nt(pick, high) + nt(pick, low)


def within_kernel(part, doc, skip, x, g, b, c, rows, cols, *refs):
    gx_out, sums_out, bc_out, u_out, w_out, heads_out, work = refs[-7:]
    heads = 2 * PART_PAIRS
    here = slice(part * heads, (part + 1) * heads)
    doc0, doc1 = doc[0, 0], doc[0, 1]
    source, target = iota((TOK, TOK), 0), iota((TOK, TOK), 1)
    seg_s = (source >= doc0).astype(jnp.int32) + (source >= doc1).astype(jnp.int32)
    seg_t = (target >= doc0).astype(jnp.int32) + (target >= doc1).astype(jnp.int32)
    mask = jnp.logical_and(target >= source, seg_s == seg_t)
    lanes = iota((TOK, 128), 1) < 64
    kern = nt(b[...], c[...])
    b_t = b[...].astype(F32).T.astype(BF16)
    c_t = c[...].astype(F32).T.astype(BF16)
    b_t = jnp.concatenate([b_t, b_t], 1)
    c_t = jnp.concatenate([c_t, c_t], 1)
    columns = cols[...]
    total, step, enter, leave = (rows[k, here, :] for k in (1, 0, 2, 3))
    last = jnp.broadcast_to(total[:, TOK - 1 :], (heads, TOK))
    timed = jnp.concatenate([enter * total, leave * step * (last - total)], 0)
    timed = jnp.concatenate([timed] * (64 // heads), 0).T
    kernel_sum = jnp.zeros((TOK, TOK), F32)
    flows, skips = [], []
    for p in range(PART_PAIRS):
        j = part * PART_PAIRS + p
        at = slice(128 * j, 128 * j + 128)
        local = slice(128 * p, 128 * p + 128)
        x_pair, g_pair = x[:, at], g[:, at]
        zero = jnp.zeros_like(x_pair)
        x_both = jnp.concatenate([jnp.where(lanes, x_pair, zero), jnp.where(lanes, zero, x_pair)], 0)
        g_both = jnp.concatenate([jnp.where(lanes, g_pair, zero), jnp.where(lanes, zero, g_pair)], 0)
        scores = nt(x_both, g_pair)
        high, low = [], []
        for i in (0, 1):
            h = 2 * j + i
            total_s = jnp.broadcast_to(columns[:, 64 + h : 65 + h], (TOK, TOK))
            step_s = jnp.broadcast_to(columns[:, 96 + h : 97 + h], (TOK, TOK))
            total_t = rows[1, h : h + 1, :]
            decay = jnp.exp(jnp.where(mask, total_t - total_s, -1e30))
            score = decay * (step_s * scores[i * TOK : (i + 1) * TOK])
            kernel_sum = kernel_sum + score
            flows.append(jnp.sum(score * kern, axis=0, keepdims=True))
            weighted = halves(decay * kern)
            high.append(weighted[0])
            low.append(weighted[1])
        inner = nn(jnp.concatenate(high, 1), g_both) + nn(jnp.concatenate(low, 1), g_both)
        x_wide, g_wide = x_pair.astype(F32), g_pair.astype(F32)
        skip_row = jnp.where(iota((1, 128), 1) < 64, skip[2 * j], skip[2 * j + 1])
        gx_out[:, local] = pair_column(columns, 96 + 2 * j, lanes) * inner + skip_row * g_wide
        work[:, local] = x_wide * inner
        skips.append(jnp.sum(x_wide * g_wide, axis=0, keepdims=True))
        timed_g = jnp.concatenate(halves(pair_column(timed, 2 * p, lanes) * g_wide), 0)
        timed_x = jnp.concatenate(halves(pair_column(timed, heads + 2 * p, lanes) * x_wide), 0)
        u_out[local, :] = nn(c_t, timed_g)
        w_out[local, :] = nn(b_t, timed_x)
    flow = jnp.concatenate(flows, 0)
    inner_x = per_head(work[...], heads)
    sums_out[0] = flow
    sums_out[1] = inner_x
    alone = jnp.sum((flow - step * inner_x) * total, axis=1, keepdims=True) / 64.0
    heads_out[:PART_PAIRS, :] = over_lanes(jnp.broadcast_to(alone, (heads, TOK)))
    heads_out[PART_PAIRS:, :] = jnp.concatenate(skips, 0)
    high, low = halves(kernel_sum)
    grad_b = nn(high, c[...]) + nn(low, c[...])
    high, low = halves(kernel_sum.T)
    grad_c = nn(high, b[...]) + nn(low, b[...])
    if part:
        grad_b = grad_b + refs[0][0]
        grad_c = grad_c + refs[0][1]
    bc_out[0] = grad_b
    bc_out[1] = grad_c


def whole_kernel(part, place, recv, u, w, kappa, heads, mine, theirs, *refs):
    entry_out, leave_out, heads_out = refs[-3:]
    core = place[0]
    terms = []
    for p in range(PART_PAIRS):
        j = part * PART_PAIRS + p
        here = slice(128 * p, 128 * p + 128)
        full = recv[here, :] + recv[PART_ROWS + p : PART_ROWS + p + 1, :] * mine[here, :]
        other = theirs[here, :]
        entry = jnp.where(core == 1, full, other)
        leave = jnp.where(core == 1, other, full)
        entry_out[here, :] = entry
        leave_out[here, :] = leave
        value = entry * (u[here, :] + kappa[j : j + 1, :] * leave) + w[here, :] * leave
        terms.append(jnp.sum(value, axis=0, keepdims=True))
    first = 2 * PART_PAIRS * part
    if part:
        heads_out[:first, :] = refs[0][...]
    heads_out[first : first + PART_PAIRS, :] = heads[:PART_PAIRS, :] + jnp.concatenate(terms, 0)
    heads_out[first + PART_PAIRS :, :] = heads[PART_PAIRS:, :]


def sums_kernel(part, x, g, cols, acc, entry_in, leave_in, bc_out):
    lanes = iota((TOK, 128), 1) < 64
    column_values = cols[...]
    grad_b, grad_c = acc[0], acc[1]
    for p in range(PART_PAIRS):
        j = part * PART_PAIRS + p
        at = slice(128 * j, 128 * j + 128)
        local = slice(128 * p, 128 * p + 128)
        entry_high, entry_low = halves(entry_in[local, :])
        leave_high, leave_low = halves(leave_in[local, :])
        x_wide, g_wide = x[:, at].astype(F32), g[:, at].astype(F32)
        high, low = halves(pair_column(column_values, 2 * j, lanes) * g_wide)
        grad_c = grad_c + nt(
            jnp.concatenate([high, low, high], 1),
            jnp.concatenate([entry_high, entry_high, entry_low], 1),
        )
        high, low = halves(pair_column(column_values, HEADS + 2 * j, lanes) * x_wide)
        grad_b = grad_b + nt(
            jnp.concatenate([high, low, high], 1),
            jnp.concatenate([leave_high, leave_high, leave_low], 1),
        )
    bc_out[0] = grad_b
    bc_out[1] = grad_c


def final_kernel(part, x, g, b, c, rows, cols, sums, gx, alog, entry_in, leave_in, *refs):
    gx_out, dt_out, work = refs[-3:]
    heads = 2 * PART_PAIRS
    first_head = part * heads
    lanes = iota((TOK, 128), 1) < 64
    column_values = cols[...]
    b_two = jnp.concatenate([b[...], b[...]], 1)
    c_two = jnp.concatenate([c[...], c[...]], 1)
    for p in range(PART_PAIRS):
        j = part * PART_PAIRS + p
        at = slice(128 * j, 128 * j + 128)
        local = slice(128 * p, 128 * p + 128)
        entry, leave = entry_in[local, :], leave_in[local, :]
        read = nn(c_two, jnp.concatenate(halves(entry), 0))
        back = nn(b_two, jnp.concatenate(halves(leave), 0))
        x_wide, g_wide = x[:, at].astype(F32), g[:, at].astype(F32)
        leave_step = pair_column(column_values, HEADS + 2 * j, lanes)
        gx_out[:, local] = (gx[:, local] + leave_step * back).astype(BF16)
        work[:TOK, local] = g_wide * read
        work[TOK : 2 * TOK, local] = x_wide * back
        work[2 * TOK :, local] = jnp.sum((entry * leave).reshape(TOK // 8, 8, 128), axis=0)
    found = per_head(work[...], heads)
    here = slice(first_head, first_head + heads)
    step, enter, leave, pre, block = (rows[k, here, :] for k in (0, 2, 3, 4, 5))
    flow, inner_x = sums[0], sums[1]
    read_g, back_x = found[:, :TOK], found[:, TOK : 2 * TOK]
    cross = jnp.sum(found[:, 2 * TOK :], axis=1, keepdims=True)
    rate = jnp.exp(column(alog[...], HEADS))[here]
    left = leave * step * back_x
    moves = flow - step * inner_x + enter * read_g - left
    end = jnp.sum(left, axis=1, keepdims=True) + cross * block[:, :1]
    from_here = (iota((TOK, TOK), 0) >= iota((TOK, TOK), 1)).astype(F32)
    decay_grad = nn(moves, from_here, HIGHEST) + end
    step_grad = inner_x + leave * back_x - rate * decay_grad
    dt_out[...] = step_grad / (1.0 + jnp.exp(-pre))


def add_kernel(*refs):
    refs[-1][...] = refs[0][...] + refs[1][...]


def heads_kernel(own, one, two, three, out):
    total = (own[...] + one[...]) + (two[...] + three[...])
    lane, head = iota((128, HEADS), 0), iota((128, HEADS), 1)
    lanes_of = (lane // 64 == head % 2).astype(F32)
    values = nn(total, lanes_of, HIGHEST)
    row, head = iota((2 * PAIRS, HEADS), 0), iota((2 * PAIRS, HEADS), 1)
    pair = row // (2 * PART_PAIRS) * PART_PAIRS + row % PART_PAIRS
    kind = row // PART_PAIRS % 2
    scale = 1.0 / math.sqrt(TOK * 32 * 64)
    for k in (0, 1):
        on = jnp.logical_and(kind == k, pair == head // 2)
        kept = jnp.where(on, values, 0.0)
        out[k : k + 1, :] = jnp.sum(kept, axis=0, keepdims=True) * scale


def join_kernel(*refs):
    gx_out, dt_out = refs[-2:]
    for part in range(PARTS):
        gx_out[:, part * PART_PAIRS * 128 : (part + 1) * PART_PAIRS * 128] = refs[part][...]
        dt_out[2 * PART_PAIRS * part : 2 * PART_PAIRS * (part + 1), :] = refs[PARTS + part][...]


def seq_pairs(move):
    pairs = []
    for y in range(ROWS):
        for z in range(CHIPS):
            for core in range(2):
                to = move(y, z, core)
                if to is not None:
                    pairs.append(
                        ((y * CHIPS + z) * 2 + core, (to[0] * CHIPS + to[1]) * 2 + to[2])
                    )
    return pairs


def other_core(value):
    return lax.ppermute(value, "seq", seq_pairs(lambda y, z, core: (y, z, 1 - core)))


def along_z(value, distance):
    return lax.ppermute(
        value, "seq", seq_pairs(lambda y, z, core: (y, (z + distance) % CHIPS, core))
    )


def along_y(value, distance):
    return lax.ppermute(
        value, "seq", seq_pairs(lambda y, z, core: ((y + distance) % ROWS, z, core))
    )


def onward_y(value, distance):
    def move(y, z, core):
        to = y + distance if core else y - distance
        return (to, z, core) if 0 <= to < ROWS else None

    return lax.ppermute(value, "seq", seq_pairs(move))


def call(kernel, ins, outs, name, scratch=(), limit=VMEM_LIMIT):
    shapes = [jax.ShapeDtypeStruct(s, d) for s, d in outs]
    return pl.pallas_call(
        kernel,
        out_shape=shapes,
        in_specs=[SPACES[space] for space, _ in ins],
        out_specs=[VMEM] * len(outs),
        scratch_shapes=list(scratch),
        name=name,
        compiler_params=pltpu.CompilerParams(vmem_limit_bytes=limit),
        cost_estimate=COST,
    )(*[value for _, value in ins])


def local(
    x_quant, scale_exp, dt_raw, dt_bias, a_log, skip_weight, b_proj, c_proj, doc_starts, grad_out
):
    index = lax.axis_index("seq")
    place = jnp.stack([index % 2, (index // 2) % CHIPS, index // (2 * CHIPS)]).astype(jnp.int32)
    alog_row = a_log.reshape(1, HEADS)
    part_shape = (PART_ROWS + 8 * -(-PART_PAIRS // 8), 128)
    chunk_shape = (CHUNK_ROWS + 8, 128)
    made = call(
        states_kernel,
        [
            (1, place),
            (1, doc_starts),
            (0, x_quant),
            (0, scale_exp),
            (0, dt_raw),
            (0, dt_bias.reshape(1, HEADS)),
            (0, alog_row),
            (0, b_proj),
            (0, c_proj),
            (0, grad_out),
        ],
        [((TOK, 2048), BF16), ((6, HEADS, TOK), F32), ((TOK, 128), F32), ((PAIRS, 128), F32)]
        + [(part_shape, F32)] * (2 * PARTS),
        "states",
    )
    x_vals, rows, cols, kappa = made[:4]
    sends, keeps = made[4 : 4 + PARTS], made[4 + PARTS :]
    recvs = [other_core(s) for s in sends]
    chunks = []
    for part in range(PARTS):
        cut = call(
            chip_kernel,
            [(1, place), (0, keeps[part]), (0, recvs[part])],
            [(chunk_shape, F32)] * CHIPS,
            "chip_total",
        )
        chunks.append([cut[0]] + [along_z(cut[CHIPS - k], -k) for k in range(1, CHIPS)])
    within = []

    def within_slab(part, after):
        made = call(
            functools.partial(within_kernel, part),
            [
                (1, doc_starts),
                (1, skip_weight),
                (0, x_vals),
                (0, grad_out),
                (0, b_proj),
                (0, c_proj),
                (0, rows),
                (0, cols),
            ]
            + [(0, v[2]) for v in within[-1:]]
            + [(2, after)],
            [
                ((TOK, PART_PAIRS * 128), F32),
                ((2, 2 * PART_PAIRS, TOK), F32),
                ((2, TOK, 128), F32),
                ((PART_ROWS, 128), F32),
                ((PART_ROWS, 128), F32),
                ((2 * PART_PAIRS, 128), F32),
            ],
            "within",
            scratch=[pltpu.VMEM((TOK, PART_PAIRS * 128), F32)],
        )
        within.append(made)

    within_slab(0, chunks[-1][0])
    row_totals = []
    for part in range(PARTS):
        (row,) = call(
            row_kernel,
            [(1, place)] + [(0, chunks[part][k]) for k in ORDER_ROW] + [(2, within[0][1] if part == 0 else rows)],
            [(chunk_shape, F32)],
            "row_total",
        )
        row_totals.append(row)
    before = [[onward_y(row, k) for k in range(1, ROWS)] for row in row_totals]
    pieces = []
    for part in range(PARTS):
        out = call(
            entry_kernel,
            [(1, place)]
            + [(0, before[part][k]) for k in ORDER_Y]
            + [(0, chunks[part][k]) for k in ORDER_ENTRY]
            + [(2, rows)],
            [((CHUNK_ROWS, 128), F32)] * CHIPS,
            "entries",
        )
        if part == 0:
            within_slab(1, out[0])
        pieces.append([out[0]] + [along_z(out[CHIPS - k], -k) for k in range(1, CHIPS)])
    gx_parts, dt_parts, finals = [], [], []

    def final(part, sums, gx, entry, leave, after):
        ins = [x_vals, grad_out, b_proj, c_proj, rows, cols, sums, gx, alog_row, entry, leave]
        return call(
            functools.partial(final_kernel, part),
            [(0, v) for v in ins] + [(2, after)],
            [((TOK, PART_PAIRS * 128), BF16), ((2 * PART_PAIRS, TOK), F32)],
            "final",
            scratch=[pltpu.VMEM((2 * TOK + 8, PART_PAIRS * 128), F32)],
        )

    bc = within[-1][2]
    heads = None
    for part in range(PARTS):
        gx, sums, _, u, w, start = within[part]
        (mine,) = call(
            assemble_kernel,
            [(1, place)] + [(0, pieces[part][k]) for k in ORDER_ASSEMBLE] + [(2, pieces[-1][0]), (2, within[part][1])],
            [((PART_ROWS, 128), F32)],
            "assemble",
        )
        theirs = other_core(mine)
        entry, leave, heads = call(
            functools.partial(whole_kernel, part),
            [(1, place)]
            + [(0, v) for v in [recvs[part], u, w, kappa, start, mine, theirs]]
            + ([(0, heads), (2, gx_parts[0])] if part else [])
            + [(2, bc)],
            [((PART_ROWS, 128), F32)] * 2 + [((2 * PART_PAIRS * (part + 1), 128), F32)],
            "whole",
        )
        (bc,) = call(
            functools.partial(sums_kernel, part),
            [(0, v) for v in [x_vals, grad_out, cols, bc, entry, leave]],
            [((2, TOK, 128), F32)],
            "sums",
        )
        if part == 0:
            gx_part, dt_part = final(part, sums, gx, entry, leave, bc)
            gx_parts.append(gx_part)
            dt_parts.append(dt_part)
        else:
            finals.append((part, sums, gx, entry, leave))
    for part, sums, gx, entry, leave in finals:
        gx_part, dt_part = final(part, sums, gx, entry, leave, bc)
        gx_parts.append(gx_part)
        dt_parts.append(dt_part)
    grad_bc = bc
    for k in range(1, 4):
        grad_bc = grad_bc + lax.ppermute(bc, "head", [(i, (i + k) % 4) for i in range(4)])
    (heads,) = call(
        add_kernel,
        [(0, heads), (0, other_core(heads)), (2, bc)],
        [((2 * PAIRS, 128), F32)],
        "chip_heads",
    )
    heads = heads + along_z(heads, 1) + along_z(heads, 2) + along_z(heads, 3)
    (head_grads,) = call(
        heads_kernel,
        [(0, heads)] + [(0, along_y(heads, k)) for k in (1, 2, 3)],
        [((2, HEADS), F32)],
        "head_grads",
    )
    grad_x, grad_dt = call(
        join_kernel,
        [(0, v) for v in gx_parts + dt_parts] + [(2, heads)],
        [((TOK, 2048), BF16), ((HEADS, TOK), F32)],
        "join",
    )
    return (grad_x, grad_dt, grad_bc, head_grads)


def solution(mesh):
    in_specs = (
        P("seq", "head"),
        P("head", "seq"),
        P("head", "seq"),
        P("head"),
        P("head"),
        P("head"),
        P("seq", None),
        P("seq", None),
        P("seq", None),
        P("seq", "head"),
    )
    out_specs = (P("seq", "head"), P("head", "seq"), P(None, "seq", None), P(None, "head"))
    return jax.shard_map(local, mesh=mesh, in_specs=in_specs, out_specs=out_specs, check_vma=False)
```

```python
import functools
import math

import jax
import jax.numpy as jnp
from jax import lax
from jax.experimental import pallas as pl
from jax.experimental.pallas import tpu as pltpu
from jax.sharding import PartitionSpec as P

F32 = jnp.float32
BF16 = jnp.bfloat16
HIGHEST = lax.Precision.HIGHEST
PARTS = 2
ROWS, CHIPS = 4, 4
TOK = 128
HEADS = 32
PAIRS = 16
PART_PAIRS = PAIRS // PARTS
CHUNK_PAIRS = PART_PAIRS // CHIPS
PART_ROWS = PART_PAIRS * TOK
CHUNK_ROWS = CHUNK_PAIRS * TOK
VMEM = pl.BlockSpec(memory_space=pltpu.VMEM)
SMEM = pl.BlockSpec(memory_space=pltpu.SMEM)
ORDER_ROW = (3, 1, 2, 0)
ORDER_ENTRY = (3, 0, 1, 2)
ORDER_ASSEMBLE = (1, 0, 2, 3)
ORDER_Y = (0, 2, 1)
ANY = pl.BlockSpec(memory_space=pl.ANY)
SPACES = (VMEM, SMEM, ANY)
VMEM_LIMIT = 24 << 20
COST = pl.CostEstimate(flops=1 << 16, bytes_accessed=1 << 12, transcendentals=0)


def nn(a, b, precision=None):
    return lax.dot_general(
        a, b, (((1,), (0,)), ((), ())), preferred_element_type=F32, precision=precision
    )


def nt(a, b, precision=None):
    return lax.dot_general(
        a, b, (((1,), (1,)), ((), ())), preferred_element_type=F32, precision=precision
    )


def halves(v):
    high = v.astype(BF16)
    return high, (v - high.astype(F32)).astype(BF16)


def iota(shape, axis):
    return lax.broadcasted_iota(jnp.int32, shape, axis)


def column(row, count):
    on = iota((count, count), 0) == iota((count, count), 1)
    return jnp.sum(jnp.where(on, jnp.broadcast_to(row, (count, count)), 0.0), axis=1, keepdims=True)


def pair_column(cols, first, lanes):
    shape = (TOK, 128)
    return jnp.where(
        lanes,
        jnp.broadcast_to(cols[:, first : first + 1], shape),
        jnp.broadcast_to(cols[:, first + 1 : first + 2], shape),
    )


def over_lanes(values):
    heads = values.shape[0]
    pick = iota((heads // 2, heads), 1) - 2 * iota((heads // 2, heads), 0)
    return jnp.where(
        iota((heads // 2, 128), 1) < 64,
        nn((pick == 0).astype(F32), values, HIGHEST),
        nn((pick == 1).astype(F32), values, HIGHEST),
    )


def states_kernel(
    place, doc, xq, scale, dt, bias, alog, b, c, g, x_out, rows_out, cols_out, kappa_out, *parts
):
    core = place[0]
    sends, keeps = parts[:PARTS], parts[PARTS:]
    doc0, doc1 = doc[0, 0], doc[0, 1]
    token = iota((HEADS, TOK), 1)
    seg = (token >= doc0).astype(jnp.int32) + (token >= doc1).astype(jnp.int32)
    seg_last = (doc0 < TOK).astype(jnp.int32) + (doc1 < TOK).astype(jnp.int32)
    pre = dt[...].astype(F32) + column(bias[...], HEADS)
    step = jnp.maximum(pre, 0.0) + jnp.log1p(jnp.exp(-jnp.abs(pre)))
    rate = jnp.exp(column(alog[...], HEADS))
    upto = (iota((TOK, TOK), 0) <= iota((TOK, TOK), 1)).astype(F32)
    total = nn(-rate * step, upto, HIGHEST)
    last = jnp.broadcast_to(total[:, TOK - 1 :], (HEADS, TOK))
    enter = jnp.where(seg == 0, jnp.exp(total), 0.0)
    leave = jnp.where(seg == seg_last, jnp.exp(last - total), 0.0)
    block = jnp.where(seg_last == 0, jnp.exp(last), 0.0)
    rows_out[0] = step
    rows_out[1] = total
    rows_out[2] = enter
    rows_out[3] = leave
    rows_out[4] = pre
    rows_out[5] = block
    cols = jnp.concatenate([enter, leave * step, total, step], 0).T
    cols_out[...] = cols
    decay = over_lanes(block)
    kappa_out[...] = decay * over_lanes(last)
    lanes = iota((TOK, 128), 1) < 64
    factor = (jnp.left_shift(jnp.int32(1), scale[...] + 8).astype(F32) / 256.0).T
    b_t = b[...].astype(F32).T.astype(BF16)
    c_t = c[...].astype(F32).T.astype(BF16)
    b_t = jnp.concatenate([b_t, b_t], 1)
    c_t = jnp.concatenate([c_t, c_t], 1)
    for j in range(0, PAIRS, 2):
        left, right = [], []
        for i in (j, j + 1):
            at = slice(128 * i, 128 * i + 128)
            x_pair = xq[:, at].astype(F32) * jnp.broadcast_to(factor[:, i : i + 1], (TOK, 128))
            x_out[:, at] = x_pair.astype(BF16)
            left.append(
                jnp.concatenate(halves(pair_column(cols, HEADS + 2 * i, lanes) * x_pair), 0)
            )
            right.append(
                jnp.concatenate(
                    halves(pair_column(cols, 2 * i, lanes) * g[:, at].astype(F32)), 0
                )
            )
        state = nn(b_t, jnp.concatenate(left, 1))
        grad = nn(c_t, jnp.concatenate(right, 1))
        part = j // PART_PAIRS
        for i in (0, 1):
            at = slice(128 * i, 128 * i + 128)
            to = slice((j + i - part * PART_PAIRS) * 128, (j + i + 1 - part * PART_PAIRS) * 128)
            sends[part][to, :] = jnp.where(core == 0, state[:, at], grad[:, at])
            keeps[part][to, :] = jnp.where(core == 0, grad[:, at], state[:, at])
    for part in range(PARTS):
        own = decay[part * PART_PAIRS : (part + 1) * PART_PAIRS]
        if PART_PAIRS < 8:
            own = jnp.concatenate([own, jnp.zeros((8 - PART_PAIRS, 128), F32)], 0)
        sends[part][PART_ROWS:, :] = own
        keeps[part][PART_ROWS:, :] = own


def chip_kernel(place, keep, recv, *outs):
    spot = place[1]
    own = keep[PART_ROWS:, :]
    both = own * recv[PART_ROWS:, :]
    for distance in range(CHIPS):
        target = (spot + distance) % CHIPS
        first = pl.multiple_of(target * CHUNK_ROWS, CHUNK_ROWS)
        decay = jnp.zeros((CHUNK_PAIRS, 128), F32)
        chip = jnp.zeros((CHUNK_PAIRS, 128), F32)
        for i in range(CHIPS):
            here = slice(i * CHUNK_PAIRS, (i + 1) * CHUNK_PAIRS)
            decay = jnp.where(target == i, own[here], decay)
            chip = jnp.where(target == i, both[here], chip)
        for p in range(CHUNK_PAIRS):
            at = pl.ds(first + p * TOK, TOK)
            outs[distance][p * TOK : (p + 1) * TOK, :] = (
                keep[at, :] + decay[p : p + 1] * recv[at, :]
            )
        outs[distance][CHUNK_ROWS:, :] = jnp.concatenate(
            [chip, jnp.zeros((8 - CHUNK_PAIRS, 128), F32)], 0
        )


def orders(place):
    spots = [(place[1] + k) % 4 for k in range(4)]
    return [jnp.where(place[0] == 1, s, 3 - s) for s in spots]


def product(decays, flags):
    weight = jnp.ones((8, 128), F32)
    for decay, flag in zip(decays, flags):
        weight = jnp.where(flag, weight * decay, weight)
    return weight


def path(order, decays, k, j):
    others = [m for m in range(4) if m != j and m != k]
    between = [jnp.logical_and(order[m] > order[k], order[m] < order[j]) for m in others]
    weight = product([decays[m] for m in others], between)
    return jnp.where(order[k] < order[j], weight, jnp.zeros((8, 128), F32))


def row_kernel(place, *refs):
    chunks, out = [refs[ORDER_ROW.index(k)] for k in range(CHIPS)], refs[-1]
    order = orders(place)
    decays = [chunk[CHUNK_ROWS:, :] for chunk in chunks]
    weights = []
    for k in range(CHIPS):
        others = [m for m in range(CHIPS) if m != k]
        weights.append(product([decays[m] for m in others], [order[m] > order[k] for m in others]))
    for p in range(CHUNK_PAIRS):
        at = slice(p * TOK, (p + 1) * TOK)
        out[at, :] = sum(weights[k][p : p + 1] * chunks[k][at, :] for k in range(CHIPS))
    out[CHUNK_ROWS:, :] = decays[0] * decays[1] * decays[2] * decays[3]


def entry_kernel(place, *refs):
    rows = [refs[ORDER_Y.index(k)] for k in range(ROWS - 1)]
    chunks = [refs[ROWS - 1 + ORDER_ENTRY.index(k)] for k in range(CHIPS)]
    outs = refs[2 * CHIPS :]
    one = rows[0][CHUNK_ROWS:, :]
    two = one * rows[1][CHUNK_ROWS:, :]
    order = orders(place)
    decays = [chunk[CHUNK_ROWS:, :] for chunk in chunks]
    weights = []
    for j in range(CHIPS):
        others = [m for m in range(CHIPS) if m != j]
        whole = product([decays[m] for m in others], [order[m] < order[j] for m in others])
        weights.append((whole, {k: path(order, decays, k, j) for k in others}))
    for p in range(CHUNK_PAIRS):
        at = slice(p * TOK, (p + 1) * TOK)
        row = rows[0][at, :] + one[p : p + 1] * rows[1][at, :] + two[p : p + 1] * rows[2][at, :]
        sources = [chunk[at, :] for chunk in chunks]
        for j in range(CHIPS):
            whole, terms = weights[j]
            value = whole[p : p + 1] * row
            for k, weight in terms.items():
                value = value + weight[p : p + 1] * sources[k]
            outs[j][at, :] = value


def assemble_kernel(place, *refs):
    out = refs[-1]
    for k in range(CHIPS):
        first = pl.multiple_of((place[1] + k) % CHIPS * CHUNK_ROWS, CHUNK_ROWS)
        out[pl.ds(first, CHUNK_ROWS), :] = refs[ORDER_ASSEMBLE.index(k)][...]


def selector(heads):
    return (iota((heads, heads * 64), 1) // 64 == iota((heads, heads * 64), 0)).astype(BF16)


def per_head(values, heads):
    high, low = halves(values)
    pick = selector(heads)
    return nt(pick, high) + nt(pick, low)


def within_kernel(part, doc, skip, x, g, b, c, rows, cols, *refs):
    gx_out, sums_out, bc_out, u_out, w_out, heads_out, work = refs[-7:]
    heads = 2 * PART_PAIRS
    here = slice(part * heads, (part + 1) * heads)
    doc0, doc1 = doc[0, 0], doc[0, 1]
    source, target = iota((TOK, TOK), 0), iota((TOK, TOK), 1)
    seg_s = (source >= doc0).astype(jnp.int32) + (source >= doc1).astype(jnp.int32)
    seg_t = (target >= doc0).astype(jnp.int32) + (target >= doc1).astype(jnp.int32)
    mask = jnp.logical_and(target >= source, seg_s == seg_t)
    lanes = iota((TOK, 128), 1) < 64
    kern = nt(b[...], c[...])
    b_t = b[...].astype(F32).T.astype(BF16)
    c_t = c[...].astype(F32).T.astype(BF16)
    b_t = jnp.concatenate([b_t, b_t], 1)
    c_t = jnp.concatenate([c_t, c_t], 1)
    columns = cols[...]
    total, step, enter, leave = (rows[k, here, :] for k in (1, 0, 2, 3))
    last = jnp.broadcast_to(total[:, TOK - 1 :], (heads, TOK))
    timed = jnp.concatenate([enter * total, leave * step * (last - total)], 0)
    timed = jnp.concatenate([timed] * (64 // heads), 0).T
    kernel_sum = jnp.zeros((TOK, TOK), F32)
    flows, skips = [], []
    for p in range(PART_PAIRS):
        j = part * PART_PAIRS + p
        at = slice(128 * j, 128 * j + 128)
        local = slice(128 * p, 128 * p + 128)
        x_pair, g_pair = x[:, at], g[:, at]
        zero = jnp.zeros_like(x_pair)
        x_both = jnp.concatenate([jnp.where(lanes, x_pair, zero), jnp.where(lanes, zero, x_pair)], 0)
        g_both = jnp.concatenate([jnp.where(lanes, g_pair, zero), jnp.where(lanes, zero, g_pair)], 0)
        scores = nt(x_both, g_pair)
        high, low = [], []
        for i in (0, 1):
            h = 2 * j + i
            total_s = jnp.broadcast_to(columns[:, 64 + h : 65 + h], (TOK, TOK))
            step_s = jnp.broadcast_to(columns[:, 96 + h : 97 + h], (TOK, TOK))
            total_t = rows[1, h : h + 1, :]
            decay = jnp.exp(jnp.where(mask, total_t - total_s, -1e30))
            score = decay * (step_s * scores[i * TOK : (i + 1) * TOK])
            kernel_sum = kernel_sum + score
            flows.append(jnp.sum(score * kern, axis=0, keepdims=True))
            weighted = halves(decay * kern)
            high.append(weighted[0])
            low.append(weighted[1])
        inner = nn(jnp.concatenate(high, 1), g_both) + nn(jnp.concatenate(low, 1), g_both)
        x_wide, g_wide = x_pair.astype(F32), g_pair.astype(F32)
        skip_row = jnp.where(iota((1, 128), 1) < 64, skip[2 * j], skip[2 * j + 1])
        gx_out[:, local] = pair_column(columns, 96 + 2 * j, lanes) * inner + skip_row * g_wide
        work[:, local] = x_wide * inner
        skips.append(jnp.sum(x_wide * g_wide, axis=0, keepdims=True))
        timed_g = jnp.concatenate(halves(pair_column(timed, 2 * p, lanes) * g_wide), 0)
        timed_x = jnp.concatenate(halves(pair_column(timed, heads + 2 * p, lanes) * x_wide), 0)
        u_out[local, :] = nn(c_t, timed_g)
        w_out[local, :] = nn(b_t, timed_x)
    flow = jnp.concatenate(flows, 0)
    inner_x = per_head(work[...], heads)
    sums_out[0] = flow
    sums_out[1] = inner_x
    alone = jnp.sum((flow - step * inner_x) * total, axis=1, keepdims=True) / 64.0
    heads_out[:PART_PAIRS, :] = over_lanes(jnp.broadcast_to(alone, (heads, TOK)))
    heads_out[PART_PAIRS:, :] = jnp.concatenate(skips, 0)
    high, low = halves(kernel_sum)
    grad_b = nn(high, c[...]) + nn(low, c[...])
    high, low = halves(kernel_sum.T)
    grad_c = nn(high, b[...]) + nn(low, b[...])
    if part:
        grad_b = grad_b + refs[0][0]
        grad_c = grad_c + refs[0][1]
    bc_out[0] = grad_b
    bc_out[1] = grad_c


def whole_kernel(part, place, recv, mine, theirs, *refs):
    entry_out, leave_out = refs[-2:]
    core = place[0]
    for p in range(PART_PAIRS):
        here = slice(128 * p, 128 * p + 128)
        full = recv[here, :] + recv[PART_ROWS + p : PART_ROWS + p + 1, :] * mine[here, :]
        other = theirs[here, :]
        entry_out[here, :] = jnp.where(core == 1, full, other)
        leave_out[here, :] = jnp.where(core == 1, other, full)


def logs_kernel(part, u, w, kappa, heads, entry_in, leave_in, *refs):
    heads_out = refs[-1]
    terms = []
    for p in range(PART_PAIRS):
        j = part * PART_PAIRS + p
        here = slice(128 * p, 128 * p + 128)
        entry, leave = entry_in[here, :], leave_in[here, :]
        value = entry * (u[here, :] + kappa[j : j + 1, :] * leave) + w[here, :] * leave
        terms.append(jnp.sum(value, axis=0, keepdims=True))
    first = 2 * PART_PAIRS * part
    if part:
        heads_out[:first, :] = refs[0][...]
    heads_out[first : first + PART_PAIRS, :] = heads[:PART_PAIRS, :] + jnp.concatenate(terms, 0)
    heads_out[first + PART_PAIRS :, :] = heads[PART_PAIRS:, :]


def sums_kernel(part, x, g, cols, acc, entry_in, leave_in, bc_out):
    lanes = iota((TOK, 128), 1) < 64
    column_values = cols[...]
    grad_b, grad_c = acc[0], acc[1]
    for p in range(PART_PAIRS):
        j = part * PART_PAIRS + p
        at = slice(128 * j, 128 * j + 128)
        local = slice(128 * p, 128 * p + 128)
        entry_high, entry_low = halves(entry_in[local, :])
        leave_high, leave_low = halves(leave_in[local, :])
        x_wide, g_wide = x[:, at].astype(F32), g[:, at].astype(F32)
        high, low = halves(pair_column(column_values, 2 * j, lanes) * g_wide)
        grad_c = grad_c + nt(
            jnp.concatenate([high, low, high], 1),
            jnp.concatenate([entry_high, entry_high, entry_low], 1),
        )
        high, low = halves(pair_column(column_values, HEADS + 2 * j, lanes) * x_wide)
        grad_b = grad_b + nt(
            jnp.concatenate([high, low, high], 1),
            jnp.concatenate([leave_high, leave_high, leave_low], 1),
        )
    bc_out[0] = grad_b
    bc_out[1] = grad_c


def final_kernel(part, x, g, b, c, rows, cols, sums, gx, alog, entry_in, leave_in, *refs):
    gx_out, dt_out, work = refs[-3:]
    heads = 2 * PART_PAIRS
    first_head = part * heads
    lanes = iota((TOK, 128), 1) < 64
    column_values = cols[...]
    b_two = jnp.concatenate([b[...], b[...]], 1)
    c_two = jnp.concatenate([c[...], c[...]], 1)
    for p in range(PART_PAIRS):
        j = part * PART_PAIRS + p
        at = slice(128 * j, 128 * j + 128)
        local = slice(128 * p, 128 * p + 128)
        entry, leave = entry_in[local, :], leave_in[local, :]
        read = nn(c_two, jnp.concatenate(halves(entry), 0))
        back = nn(b_two, jnp.concatenate(halves(leave), 0))
        x_wide, g_wide = x[:, at].astype(F32), g[:, at].astype(F32)
        leave_step = pair_column(column_values, HEADS + 2 * j, lanes)
        gx_out[:, local] = (gx[:, local] + leave_step * back).astype(BF16)
        work[:TOK, local] = g_wide * read
        work[TOK : 2 * TOK, local] = x_wide * back
        work[2 * TOK :, local] = jnp.sum((entry * leave).reshape(TOK // 8, 8, 128), axis=0)
    found = per_head(work[...], heads)
    here = slice(first_head, first_head + heads)
    step, enter, leave, pre, block = (rows[k, here, :] for k in (0, 2, 3, 4, 5))
    flow, inner_x = sums[0], sums[1]
    read_g, back_x = found[:, :TOK], found[:, TOK : 2 * TOK]
    cross = jnp.sum(found[:, 2 * TOK :], axis=1, keepdims=True)
    rate = jnp.exp(column(alog[...], HEADS))[here]
    left = leave * step * back_x
    moves = flow - step * inner_x + enter * read_g - left
    end = jnp.sum(left, axis=1, keepdims=True) + cross * block[:, :1]
    from_here = (iota((TOK, TOK), 0) >= iota((TOK, TOK), 1)).astype(F32)
    decay_grad = nn(moves, from_here, HIGHEST) + end
    step_grad = inner_x + leave * back_x - rate * decay_grad
    dt_out[...] = step_grad / (1.0 + jnp.exp(-pre))


def add_kernel(*refs):
    refs[-1][...] = refs[0][...] + refs[1][...]


def heads_kernel(own, one, two, three, bc, bc_one, bc_two, bc_three, out, bc_out):
    bc_out[...] = (bc[...] + bc_one[...]) + (bc_two[...] + bc_three[...])
    total = (own[...] + one[...]) + (two[...] + three[...])
    lane, head = iota((128, HEADS), 0), iota((128, HEADS), 1)
    lanes_of = (lane // 64 == head % 2).astype(F32)
    values = nn(total, lanes_of, HIGHEST)
    row, head = iota((2 * PAIRS, HEADS), 0), iota((2 * PAIRS, HEADS), 1)
    pair = row // (2 * PART_PAIRS) * PART_PAIRS + row % PART_PAIRS
    kind = row // PART_PAIRS % 2
    scale = 1.0 / math.sqrt(TOK * 32 * 64)
    for k in (0, 1):
        on = jnp.logical_and(kind == k, pair == head // 2)
        kept = jnp.where(on, values, 0.0)
        out[k : k + 1, :] = jnp.sum(kept, axis=0, keepdims=True) * scale


def join_kernel(*refs):
    gx_out, dt_out = refs[-2:]
    for part in range(PARTS):
        gx_out[:, part * PART_PAIRS * 128 : (part + 1) * PART_PAIRS * 128] = refs[part][...]
        dt_out[2 * PART_PAIRS * part : 2 * PART_PAIRS * (part + 1), :] = refs[PARTS + part][...]


def seq_pairs(move):
    pairs = []
    for y in range(ROWS):
        for z in range(CHIPS):
            for core in range(2):
                to = move(y, z, core)
                if to is not None:
                    pairs.append(
                        ((y * CHIPS + z) * 2 + core, (to[0] * CHIPS + to[1]) * 2 + to[2])
                    )
    return pairs


def other_core(value):
    return lax.ppermute(value, "seq", seq_pairs(lambda y, z, core: (y, z, 1 - core)))


def along_z(value, distance):
    return lax.ppermute(
        value, "seq", seq_pairs(lambda y, z, core: (y, (z + distance) % CHIPS, core))
    )


def along_y(value, distance):
    return lax.ppermute(
        value, "seq", seq_pairs(lambda y, z, core: ((y + distance) % ROWS, z, core))
    )


def onward_y(value, distance):
    def move(y, z, core):
        to = y + distance if core else y - distance
        return (to, z, core) if 0 <= to < ROWS else None

    return lax.ppermute(value, "seq", seq_pairs(move))


def call(kernel, ins, outs, name, scratch=(), limit=VMEM_LIMIT):
    shapes = [jax.ShapeDtypeStruct(s, d) for s, d in outs]
    return pl.pallas_call(
        kernel,
        out_shape=shapes,
        in_specs=[SPACES[space] for space, _ in ins],
        out_specs=[VMEM] * len(outs),
        scratch_shapes=list(scratch),
        name=name,
        compiler_params=pltpu.CompilerParams(vmem_limit_bytes=limit),
        cost_estimate=COST,
    )(*[value for _, value in ins])


def local(
    x_quant, scale_exp, dt_raw, dt_bias, a_log, skip_weight, b_proj, c_proj, doc_starts, grad_out
):
    index = lax.axis_index("seq")
    place = jnp.stack([index % 2, (index // 2) % CHIPS, index // (2 * CHIPS)]).astype(jnp.int32)
    alog_row = a_log.reshape(1, HEADS)
    part_shape = (PART_ROWS + 8 * -(-PART_PAIRS // 8), 128)
    chunk_shape = (CHUNK_ROWS + 8, 128)
    made = call(
        states_kernel,
        [
            (1, place),
            (1, doc_starts),
            (0, x_quant),
            (0, scale_exp),
            (0, dt_raw),
            (0, dt_bias.reshape(1, HEADS)),
            (0, alog_row),
            (0, b_proj),
            (0, c_proj),
            (0, grad_out),
        ],
        [((TOK, 2048), BF16), ((6, HEADS, TOK), F32), ((TOK, 128), F32), ((PAIRS, 128), F32)]
        + [(part_shape, F32)] * (2 * PARTS),
        "states",
    )
    x_vals, rows, cols, kappa = made[:4]
    sends, keeps = made[4 : 4 + PARTS], made[4 + PARTS :]
    recvs = [other_core(s) for s in sends]
    chunks = []
    for part in range(PARTS):
        cut = call(
            chip_kernel,
            [(1, place), (0, keeps[part]), (0, recvs[part])],
            [(chunk_shape, F32)] * CHIPS,
            "chip_total",
        )
        chunks.append([cut[0]] + [along_z(cut[CHIPS - k], -k) for k in range(1, CHIPS)])
    within = []

    def within_slab(part, after):
        made = call(
            functools.partial(within_kernel, part),
            [
                (1, doc_starts),
                (1, skip_weight),
                (0, x_vals),
                (0, grad_out),
                (0, b_proj),
                (0, c_proj),
                (0, rows),
                (0, cols),
            ]
            + [(0, v[2]) for v in within[-1:]]
            + [(2, after)],
            [
                ((TOK, PART_PAIRS * 128), F32),
                ((2, 2 * PART_PAIRS, TOK), F32),
                ((2, TOK, 128), F32),
                ((PART_ROWS, 128), F32),
                ((PART_ROWS, 128), F32),
                ((2 * PART_PAIRS, 128), F32),
            ],
            "within",
            scratch=[pltpu.VMEM((TOK, PART_PAIRS * 128), F32)],
        )
        within.append(made)

    within_slab(0, chunks[-1][0])
    row_totals = []
    for part in range(PARTS):
        (row,) = call(
            row_kernel,
            [(1, place)] + [(0, chunks[part][k]) for k in ORDER_ROW] + [(2, within[0][1] if part == 0 else rows)],
            [(chunk_shape, F32)],
            "row_total",
        )
        row_totals.append(row)
    before = [[onward_y(row, k) for k in range(1, ROWS)] for row in row_totals]
    pieces = []
    for part in range(PARTS):
        out = call(
            entry_kernel,
            [(1, place)]
            + [(0, before[part][k]) for k in ORDER_Y]
            + [(0, chunks[part][k]) for k in ORDER_ENTRY]
            + [(2, rows)],
            [((CHUNK_ROWS, 128), F32)] * CHIPS,
            "entries",
        )
        if part == 0:
            within_slab(1, out[0])
        pieces.append([out[0]] + [along_z(out[CHIPS - k], -k) for k in range(1, CHIPS)])
    gx_parts, dt_parts, finals = [], [], []

    def final(part, sums, gx, entry, leave, after):
        ins = [x_vals, grad_out, b_proj, c_proj, rows, cols, sums, gx, alog_row, entry, leave]
        return call(
            functools.partial(final_kernel, part),
            [(0, v) for v in ins] + [(2, after)],
            [((TOK, PART_PAIRS * 128), BF16), ((2 * PART_PAIRS, TOK), F32)],
            "final",
            scratch=[pltpu.VMEM((2 * TOK + 8, PART_PAIRS * 128), F32)],
        )

    bc = within[-1][2]
    heads = None
    for part in range(PARTS):
        gx, sums, _, u, w, start = within[part]
        (mine,) = call(
            assemble_kernel,
            [(1, place)] + [(0, pieces[part][k]) for k in ORDER_ASSEMBLE] + [(2, pieces[-1][0]), (2, within[part][1])],
            [((PART_ROWS, 128), F32)],
            "assemble",
        )
        theirs = other_core(mine)
        entry, leave = call(
            functools.partial(whole_kernel, part),
            [(1, place), (0, recvs[part]), (0, mine), (0, theirs)]
            + [(2, bc)],
            [((PART_ROWS, 128), F32)] * 2,
            "whole",
        )
        (bc,) = call(
            functools.partial(sums_kernel, part),
            [(0, v) for v in [x_vals, grad_out, cols, bc, entry, leave]],
            [((2, TOK, 128), F32)],
            "sums",
        )
        (heads,) = call(
            functools.partial(logs_kernel, part),
            [(0, v) for v in [u, w, kappa, start, entry, leave]]
            + ([(0, heads)] if part else [])
            + [(2, bc)],
            [((2 * PART_PAIRS * (part + 1), 128), F32)],
            "logs",
        )
        if part == 0:
            gx_part, dt_part = final(part, sums, gx, entry, leave, bc)
            gx_parts.append(gx_part)
            dt_parts.append(dt_part)
        else:
            finals.append((part, sums, gx, entry, leave))
    for part, sums, gx, entry, leave in finals:
        gx_part, dt_part = final(part, sums, gx, entry, leave, bc)
        gx_parts.append(gx_part)
        dt_parts.append(dt_part)
    others = [lax.ppermute(bc, "head", [(i, (i + k) % 4) for i in range(4)]) for k in (1, 2, 3)]
    (heads,) = call(
        add_kernel,
        [(0, heads), (0, other_core(heads)), (2, bc)],
        [((2 * PAIRS, 128), F32)],
        "chip_heads",
    )
    heads = heads + along_z(heads, 1) + along_z(heads, 2) + along_z(heads, 3)
    head_grads, grad_bc = call(
        heads_kernel,
        [(0, heads)] + [(0, along_y(heads, k)) for k in (1, 2, 3)] + [(0, v) for v in [bc] + others],
        [((2, HEADS), F32), ((2, TOK, 128), F32)],
        "last",
    )
    grad_x, grad_dt = call(
        join_kernel,
        [(0, v) for v in gx_parts + dt_parts] + [(2, heads)],
        [((TOK, 2048), BF16), ((HEADS, TOK), F32)],
        "join",
    )
    return (grad_x, grad_dt, grad_bc, head_grads)


def solution(mesh):
    in_specs = (
        P("seq", "head"),
        P("head", "seq"),
        P("head", "seq"),
        P("head"),
        P("head"),
        P("head"),
        P("seq", None),
        P("seq", None),
        P("seq", None),
        P("seq", "head"),
    )
    out_specs = (P("seq", "head"), P("head", "seq"), P(None, "seq", None), P(None, "head"))
    return jax.shard_map(local, mesh=mesh, in_specs=in_specs, out_specs=out_specs, check_vma=False)
```

```python
import functools
import math

import jax
import jax.numpy as jnp
from jax import lax
from jax.experimental import pallas as pl
from jax.experimental.pallas import tpu as pltpu
from jax.sharding import PartitionSpec as P

F32 = jnp.float32
BF16 = jnp.bfloat16
HIGHEST = lax.Precision.HIGHEST
PARTS = 2
ROWS, CHIPS = 4, 4
TOK = 128
HEADS = 32
PAIRS = 16
PART_PAIRS = PAIRS // PARTS
CHUNK_PAIRS = PART_PAIRS // CHIPS
PART_ROWS = PART_PAIRS * TOK
CHUNK_ROWS = CHUNK_PAIRS * TOK
VMEM = pl.BlockSpec(memory_space=pltpu.VMEM)
SMEM = pl.BlockSpec(memory_space=pltpu.SMEM)
ORDER_ROW = (3, 1, 2, 0)
ORDER_ENTRY = (3, 2, 1, 0)
ORDER_ASSEMBLE = (2, 1, 3, 0)
ORDER_Y = (0, 1, 2)
ANY = pl.BlockSpec(memory_space=pl.ANY)
SPACES = (VMEM, SMEM, ANY)
VMEM_LIMIT = 24 << 20
COST = pl.CostEstimate(flops=1 << 16, bytes_accessed=1 << 12, transcendentals=0)


def nn(a, b, precision=None):
    return lax.dot_general(
        a, b, (((1,), (0,)), ((), ())), preferred_element_type=F32, precision=precision
    )


def nt(a, b, precision=None):
    return lax.dot_general(
        a, b, (((1,), (1,)), ((), ())), preferred_element_type=F32, precision=precision
    )


def halves(v):
    high = v.astype(BF16)
    return high, (v - high.astype(F32)).astype(BF16)


def iota(shape, axis):
    return lax.broadcasted_iota(jnp.int32, shape, axis)


def column(row, count):
    on = iota((count, count), 0) == iota((count, count), 1)
    return jnp.sum(jnp.where(on, jnp.broadcast_to(row, (count, count)), 0.0), axis=1, keepdims=True)


def pair_column(cols, first, lanes):
    shape = (TOK, 128)
    return jnp.where(
        lanes,
        jnp.broadcast_to(cols[:, first : first + 1], shape),
        jnp.broadcast_to(cols[:, first + 1 : first + 2], shape),
    )


def over_lanes(values):
    heads = values.shape[0]
    pick = iota((heads // 2, heads), 1) - 2 * iota((heads // 2, heads), 0)
    return jnp.where(
        iota((heads // 2, 128), 1) < 64,
        nn((pick == 0).astype(F32), values, HIGHEST),
        nn((pick == 1).astype(F32), values, HIGHEST),
    )


def states_kernel(
    place, doc, xq, scale, dt, bias, alog, b, c, g, x_out, rows_out, cols_out, kappa_out, *parts
):
    core = place[0]
    sends, keeps = parts[:PARTS], parts[PARTS:]
    doc0, doc1 = doc[0, 0], doc[0, 1]
    token = iota((HEADS, TOK), 1)
    seg = (token >= doc0).astype(jnp.int32) + (token >= doc1).astype(jnp.int32)
    seg_last = (doc0 < TOK).astype(jnp.int32) + (doc1 < TOK).astype(jnp.int32)
    pre = dt[...].astype(F32) + column(bias[...], HEADS)
    step = jnp.maximum(pre, 0.0) + jnp.log1p(jnp.exp(-jnp.abs(pre)))
    rate = jnp.exp(column(alog[...], HEADS))
    upto = (iota((TOK, TOK), 0) <= iota((TOK, TOK), 1)).astype(F32)
    total = nn(-rate * step, upto, HIGHEST)
    last = jnp.broadcast_to(total[:, TOK - 1 :], (HEADS, TOK))
    enter = jnp.where(seg == 0, jnp.exp(total), 0.0)
    leave = jnp.where(seg == seg_last, jnp.exp(last - total), 0.0)
    block = jnp.where(seg_last == 0, jnp.exp(last), 0.0)
    rows_out[0] = step
    rows_out[1] = total
    rows_out[2] = enter
    rows_out[3] = leave
    rows_out[4] = pre
    rows_out[5] = block
    cols = jnp.concatenate([enter, leave * step, total, step], 0).T
    cols_out[...] = cols
    decay = over_lanes(block)
    kappa_out[...] = decay * over_lanes(last)
    lanes = iota((TOK, 128), 1) < 64
    factor = (jnp.left_shift(jnp.int32(1), scale[...] + 8).astype(F32) / 256.0).T
    b_t = b[...].astype(F32).T.astype(BF16)
    c_t = c[...].astype(F32).T.astype(BF16)
    b_t = jnp.concatenate([b_t, b_t], 1)
    c_t = jnp.concatenate([c_t, c_t], 1)
    for j in range(0, PAIRS, 2):
        left, right = [], []
        for i in (j, j + 1):
            at = slice(128 * i, 128 * i + 128)
            x_pair = xq[:, at].astype(F32) * jnp.broadcast_to(factor[:, i : i + 1], (TOK, 128))
            x_out[:, at] = x_pair.astype(BF16)
            left.append(
                jnp.concatenate(halves(pair_column(cols, HEADS + 2 * i, lanes) * x_pair), 0)
            )
            right.append(
                jnp.concatenate(
                    halves(pair_column(cols, 2 * i, lanes) * g[:, at].astype(F32)), 0
                )
            )
        state = nn(b_t, jnp.concatenate(left, 1))
        grad = nn(c_t, jnp.concatenate(right, 1))
        part = j // PART_PAIRS
        for i in (0, 1):
            at = slice(128 * i, 128 * i + 128)
            to = slice((j + i - part * PART_PAIRS) * 128, (j + i + 1 - part * PART_PAIRS) * 128)
            sends[part][to, :] = jnp.where(core == 0, state[:, at], grad[:, at])
            keeps[part][to, :] = jnp.where(core == 0, grad[:, at], state[:, at])
    for part in range(PARTS):
        own = decay[part * PART_PAIRS : (part + 1) * PART_PAIRS]
        if PART_PAIRS < 8:
            own = jnp.concatenate([own, jnp.zeros((8 - PART_PAIRS, 128), F32)], 0)
        sends[part][PART_ROWS:, :] = own
        keeps[part][PART_ROWS:, :] = own


def chip_kernel(place, keep, recv, *outs):
    spot = place[1]
    own = keep[PART_ROWS:, :]
    both = own * recv[PART_ROWS:, :]
    for distance in range(CHIPS):
        target = (spot + distance) % CHIPS
        first = pl.multiple_of(target * CHUNK_ROWS, CHUNK_ROWS)
        decay = jnp.zeros((CHUNK_PAIRS, 128), F32)
        chip = jnp.zeros((CHUNK_PAIRS, 128), F32)
        for i in range(CHIPS):
            here = slice(i * CHUNK_PAIRS, (i + 1) * CHUNK_PAIRS)
            decay = jnp.where(target == i, own[here], decay)
            chip = jnp.where(target == i, both[here], chip)
        for p in range(CHUNK_PAIRS):
            at = pl.ds(first + p * TOK, TOK)
            outs[distance][p * TOK : (p + 1) * TOK, :] = (
                keep[at, :] + decay[p : p + 1] * recv[at, :]
            )
        outs[distance][CHUNK_ROWS:, :] = jnp.concatenate(
            [chip, jnp.zeros((8 - CHUNK_PAIRS, 128), F32)], 0
        )


def orders(place):
    spots = [(place[1] + k) % 4 for k in range(4)]
    return [jnp.where(place[0] == 1, s, 3 - s) for s in spots]


def product(decays, flags):
    weight = jnp.ones((8, 128), F32)
    for decay, flag in zip(decays, flags):
        weight = jnp.where(flag, weight * decay, weight)
    return weight


def path(order, decays, k, j):
    others = [m for m in range(4) if m != j and m != k]
    between = [jnp.logical_and(order[m] > order[k], order[m] < order[j]) for m in others]
    weight = product([decays[m] for m in others], between)
    return jnp.where(order[k] < order[j], weight, jnp.zeros((8, 128), F32))


def row_kernel(place, *refs):
    chunks, out = [refs[ORDER_ROW.index(k)] for k in range(CHIPS)], refs[-1]
    order = orders(place)
    decays = [chunk[CHUNK_ROWS:, :] for chunk in chunks]
    weights = []
    for k in range(CHIPS):
        others = [m for m in range(CHIPS) if m != k]
        weights.append(product([decays[m] for m in others], [order[m] > order[k] for m in others]))
    for p in range(CHUNK_PAIRS):
        at = slice(p * TOK, (p + 1) * TOK)
        out[at, :] = sum(weights[k][p : p + 1] * chunks[k][at, :] for k in range(CHIPS))
    out[CHUNK_ROWS:, :] = decays[0] * decays[1] * decays[2] * decays[3]


def entry_kernel(place, *refs):
    rows = [refs[ORDER_Y.index(k)] for k in range(ROWS - 1)]
    chunks = [refs[ROWS - 1 + ORDER_ENTRY.index(k)] for k in range(CHIPS)]
    outs = refs[2 * CHIPS :]
    one = rows[0][CHUNK_ROWS:, :]
    two = one * rows[1][CHUNK_ROWS:, :]
    order = orders(place)
    decays = [chunk[CHUNK_ROWS:, :] for chunk in chunks]
    weights = []
    for j in range(CHIPS):
        others = [m for m in range(CHIPS) if m != j]
        whole = product([decays[m] for m in others], [order[m] < order[j] for m in others])
        weights.append((whole, {k: path(order, decays, k, j) for k in others}))
    for p in range(CHUNK_PAIRS):
        at = slice(p * TOK, (p + 1) * TOK)
        row = rows[0][at, :] + one[p : p + 1] * rows[1][at, :] + two[p : p + 1] * rows[2][at, :]
        sources = [chunk[at, :] for chunk in chunks]
        for j in range(CHIPS):
            whole, terms = weights[j]
            value = whole[p : p + 1] * row
            for k, weight in terms.items():
                value = value + weight[p : p + 1] * sources[k]
            outs[j][at, :] = value


def assemble_kernel(place, *refs):
    out = refs[-1]
    for k in range(CHIPS):
        first = pl.multiple_of((place[1] + k) % CHIPS * CHUNK_ROWS, CHUNK_ROWS)
        out[pl.ds(first, CHUNK_ROWS), :] = refs[ORDER_ASSEMBLE.index(k)][...]


def selector(heads):
    return (iota((heads, heads * 64), 1) // 64 == iota((heads, heads * 64), 0)).astype(BF16)


def per_head(values, heads):
    high, low = halves(values)
    pick = selector(heads)
    return nt(pick, high) + nt(pick, low)


def within_kernel(part, doc, skip, x, g, b, c, rows, cols, *refs):
    gx_out, sums_out, bc_out, u_out, w_out, heads_out, work = refs[-7:]
    heads = 2 * PART_PAIRS
    here = slice(part * heads, (part + 1) * heads)
    doc0, doc1 = doc[0, 0], doc[0, 1]
    source, target = iota((TOK, TOK), 0), iota((TOK, TOK), 1)
    seg_s = (source >= doc0).astype(jnp.int32) + (source >= doc1).astype(jnp.int32)
    seg_t = (target >= doc0).astype(jnp.int32) + (target >= doc1).astype(jnp.int32)
    mask = jnp.logical_and(target >= source, seg_s == seg_t)
    lanes = iota((TOK, 128), 1) < 64
    kern = nt(b[...], c[...])
    b_t = b[...].astype(F32).T.astype(BF16)
    c_t = c[...].astype(F32).T.astype(BF16)
    b_t = jnp.concatenate([b_t, b_t], 1)
    c_t = jnp.concatenate([c_t, c_t], 1)
    columns = cols[...]
    total, step, enter, leave = (rows[k, here, :] for k in (1, 0, 2, 3))
    last = jnp.broadcast_to(total[:, TOK - 1 :], (heads, TOK))
    timed = jnp.concatenate([enter * total, leave * step * (last - total)], 0)
    timed = jnp.concatenate([timed] * (64 // heads), 0).T
    kernel_sum = jnp.zeros((TOK, TOK), F32)
    flows, skips = [], []
    for p in range(PART_PAIRS):
        j = part * PART_PAIRS + p
        at = slice(128 * j, 128 * j + 128)
        local = slice(128 * p, 128 * p + 128)
        x_pair, g_pair = x[:, at], g[:, at]
        zero = jnp.zeros_like(x_pair)
        x_both = jnp.concatenate([jnp.where(lanes, x_pair, zero), jnp.where(lanes, zero, x_pair)], 0)
        g_both = jnp.concatenate([jnp.where(lanes, g_pair, zero), jnp.where(lanes, zero, g_pair)], 0)
        scores = nt(x_both, g_pair)
        high, low = [], []
        for i in (0, 1):
            h = 2 * j + i
            total_s = jnp.broadcast_to(columns[:, 64 + h : 65 + h], (TOK, TOK))
            step_s = jnp.broadcast_to(columns[:, 96 + h : 97 + h], (TOK, TOK))
            total_t = rows[1, h : h + 1, :]
            decay = jnp.exp(jnp.where(mask, total_t - total_s, -1e30))
            score = decay * (step_s * scores[i * TOK : (i + 1) * TOK])
            kernel_sum = kernel_sum + score
            flows.append(jnp.sum(score * kern, axis=0, keepdims=True))
            weighted = halves(decay * kern)
            high.append(weighted[0])
            low.append(weighted[1])
        inner = nn(jnp.concatenate(high, 1), g_both) + nn(jnp.concatenate(low, 1), g_both)
        x_wide, g_wide = x_pair.astype(F32), g_pair.astype(F32)
        skip_row = jnp.where(iota((1, 128), 1) < 64, skip[2 * j], skip[2 * j + 1])
        gx_out[:, local] = pair_column(columns, 96 + 2 * j, lanes) * inner + skip_row * g_wide
        work[:, local] = x_wide * inner
        skips.append(jnp.sum(x_wide * g_wide, axis=0, keepdims=True))
        timed_g = jnp.concatenate(halves(pair_column(timed, 2 * p, lanes) * g_wide), 0)
        timed_x = jnp.concatenate(halves(pair_column(timed, heads + 2 * p, lanes) * x_wide), 0)
        u_out[local, :] = nn(c_t, timed_g)
        w_out[local, :] = nn(b_t, timed_x)
    flow = jnp.concatenate(flows, 0)
    inner_x = per_head(work[...], heads)
    sums_out[0] = flow
    sums_out[1] = inner_x
    alone = jnp.sum((flow - step * inner_x) * total, axis=1, keepdims=True) / 64.0
    heads_out[:PART_PAIRS, :] = over_lanes(jnp.broadcast_to(alone, (heads, TOK)))
    heads_out[PART_PAIRS:, :] = jnp.concatenate(skips, 0)
    high, low = halves(kernel_sum)
    grad_b = nn(high, c[...]) + nn(low, c[...])
    high, low = halves(kernel_sum.T)
    grad_c = nn(high, b[...]) + nn(low, b[...])
    if part:
        grad_b = grad_b + refs[0][0]
        grad_c = grad_c + refs[0][1]
    bc_out[0] = grad_b
    bc_out[1] = grad_c


def whole_kernel(part, place, recv, mine, theirs, *refs):
    entry_out, leave_out = refs[-2:]
    core = place[0]
    for p in range(PART_PAIRS):
        here = slice(128 * p, 128 * p + 128)
        full = recv[here, :] + recv[PART_ROWS + p : PART_ROWS + p + 1, :] * mine[here, :]
        other = theirs[here, :]
        entry_out[here, :] = jnp.where(core == 1, full, other)
        leave_out[here, :] = jnp.where(core == 1, other, full)


def logs_kernel(part, u, w, kappa, heads, entry_in, leave_in, *refs):
    heads_out = refs[-1]
    terms = []
    for p in range(PART_PAIRS):
        j = part * PART_PAIRS + p
        here = slice(128 * p, 128 * p + 128)
        entry, leave = entry_in[here, :], leave_in[here, :]
        value = entry * (u[here, :] + kappa[j : j + 1, :] * leave) + w[here, :] * leave
        terms.append(jnp.sum(value, axis=0, keepdims=True))
    first = 2 * PART_PAIRS * part
    if part:
        heads_out[:first, :] = refs[0][...]
    heads_out[first : first + PART_PAIRS, :] = heads[:PART_PAIRS, :] + jnp.concatenate(terms, 0)
    heads_out[first + PART_PAIRS :, :] = heads[PART_PAIRS:, :]


def sums_kernel(part, x, g, cols, acc, entry_in, leave_in, bc_out):
    lanes = iota((TOK, 128), 1) < 64
    column_values = cols[...]
    grad_b, grad_c = acc[0], acc[1]
    for p in range(PART_PAIRS):
        j = part * PART_PAIRS + p
        at = slice(128 * j, 128 * j + 128)
        local = slice(128 * p, 128 * p + 128)
        entry_high, entry_low = halves(entry_in[local, :])
        leave_high, leave_low = halves(leave_in[local, :])
        x_wide, g_wide = x[:, at].astype(F32), g[:, at].astype(F32)
        high, low = halves(pair_column(column_values, 2 * j, lanes) * g_wide)
        grad_c = grad_c + nt(
            jnp.concatenate([high, low, high], 1),
            jnp.concatenate([entry_high, entry_high, entry_low], 1),
        )
        high, low = halves(pair_column(column_values, HEADS + 2 * j, lanes) * x_wide)
        grad_b = grad_b + nt(
            jnp.concatenate([high, low, high], 1),
            jnp.concatenate([leave_high, leave_high, leave_low], 1),
        )
    bc_out[0] = grad_b
    bc_out[1] = grad_c


def final_kernel(part, x, g, b, c, rows, cols, sums, gx, alog, entry_in, leave_in, *refs):
    gx_out, dt_out, work = refs[-3:]
    heads = 2 * PART_PAIRS
    first_head = part * heads
    lanes = iota((TOK, 128), 1) < 64
    column_values = cols[...]
    b_two = jnp.concatenate([b[...], b[...]], 1)
    c_two = jnp.concatenate([c[...], c[...]], 1)
    for p in range(PART_PAIRS):
        j = part * PART_PAIRS + p
        at = slice(128 * j, 128 * j + 128)
        local = slice(128 * p, 128 * p + 128)
        entry, leave = entry_in[local, :], leave_in[local, :]
        read = nn(c_two, jnp.concatenate(halves(entry), 0))
        back = nn(b_two, jnp.concatenate(halves(leave), 0))
        x_wide, g_wide = x[:, at].astype(F32), g[:, at].astype(F32)
        leave_step = pair_column(column_values, HEADS + 2 * j, lanes)
        gx_out[:, local] = (gx[:, local] + leave_step * back).astype(BF16)
        work[:TOK, local] = g_wide * read
        work[TOK : 2 * TOK, local] = x_wide * back
        work[2 * TOK :, local] = jnp.sum((entry * leave).reshape(TOK // 8, 8, 128), axis=0)
    found = per_head(work[...], heads)
    here = slice(first_head, first_head + heads)
    step, enter, leave, pre, block = (rows[k, here, :] for k in (0, 2, 3, 4, 5))
    flow, inner_x = sums[0], sums[1]
    read_g, back_x = found[:, :TOK], found[:, TOK : 2 * TOK]
    cross = jnp.sum(found[:, 2 * TOK :], axis=1, keepdims=True)
    rate = jnp.exp(column(alog[...], HEADS))[here]
    left = leave * step * back_x
    moves = flow - step * inner_x + enter * read_g - left
    end = jnp.sum(left, axis=1, keepdims=True) + cross * block[:, :1]
    from_here = (iota((TOK, TOK), 0) >= iota((TOK, TOK), 1)).astype(F32)
    decay_grad = nn(moves, from_here, HIGHEST) + end
    step_grad = inner_x + leave * back_x - rate * decay_grad
    dt_out[...] = step_grad / (1.0 + jnp.exp(-pre))


def add_kernel(*refs):
    refs[-1][...] = refs[0][...] + refs[1][...]


def heads_kernel(own, one, two, three, bc, bc_one, bc_two, bc_three, out, bc_out):
    bc_out[...] = (bc[...] + bc_one[...]) + (bc_two[...] + bc_three[...])
    total = (own[...] + one[...]) + (two[...] + three[...])
    lane, head = iota((128, HEADS), 0), iota((128, HEADS), 1)
    lanes_of = (lane // 64 == head % 2).astype(F32)
    values = nn(total, lanes_of, HIGHEST)
    row, head = iota((2 * PAIRS, HEADS), 0), iota((2 * PAIRS, HEADS), 1)
    pair = row // (2 * PART_PAIRS) * PART_PAIRS + row % PART_PAIRS
    kind = row // PART_PAIRS % 2
    scale = 1.0 / math.sqrt(TOK * 32 * 64)
    for k in (0, 1):
        on = jnp.logical_and(kind == k, pair == head // 2)
        kept = jnp.where(on, values, 0.0)
        out[k : k + 1, :] = jnp.sum(kept, axis=0, keepdims=True) * scale


def join_kernel(*refs):
    gx_out, dt_out = refs[-2:]
    for part in range(PARTS):
        gx_out[:, part * PART_PAIRS * 128 : (part + 1) * PART_PAIRS * 128] = refs[part][...]
        dt_out[2 * PART_PAIRS * part : 2 * PART_PAIRS * (part + 1), :] = refs[PARTS + part][...]


def seq_pairs(move):
    pairs = []
    for y in range(ROWS):
        for z in range(CHIPS):
            for core in range(2):
                to = move(y, z, core)
                if to is not None:
                    pairs.append(
                        ((y * CHIPS + z) * 2 + core, (to[0] * CHIPS + to[1]) * 2 + to[2])
                    )
    return pairs


def other_core(value):
    return lax.ppermute(value, "seq", seq_pairs(lambda y, z, core: (y, z, 1 - core)))


def along_z(value, distance):
    return lax.ppermute(
        value, "seq", seq_pairs(lambda y, z, core: (y, (z + distance) % CHIPS, core))
    )


def along_y(value, distance):
    return lax.ppermute(
        value, "seq", seq_pairs(lambda y, z, core: ((y + distance) % ROWS, z, core))
    )


def onward_y(value, distance):
    def move(y, z, core):
        to = y + distance if core else y - distance
        return (to, z, core) if 0 <= to < ROWS else None

    return lax.ppermute(value, "seq", seq_pairs(move))


def call(kernel, ins, outs, name, scratch=(), limit=VMEM_LIMIT):
    shapes = [jax.ShapeDtypeStruct(s, d) for s, d in outs]
    return pl.pallas_call(
        kernel,
        out_shape=shapes,
        in_specs=[SPACES[space] for space, _ in ins],
        out_specs=[VMEM] * len(outs),
        scratch_shapes=list(scratch),
        name=name,
        compiler_params=pltpu.CompilerParams(vmem_limit_bytes=limit),
        cost_estimate=COST,
    )(*[value for _, value in ins])


def local(
    x_quant, scale_exp, dt_raw, dt_bias, a_log, skip_weight, b_proj, c_proj, doc_starts, grad_out
):
    index = lax.axis_index("seq")
    place = jnp.stack([index % 2, (index // 2) % CHIPS, index // (2 * CHIPS)]).astype(jnp.int32)
    alog_row = a_log.reshape(1, HEADS)
    part_shape = (PART_ROWS + 8 * -(-PART_PAIRS // 8), 128)
    chunk_shape = (CHUNK_ROWS + 8, 128)
    made = call(
        states_kernel,
        [
            (1, place),
            (1, doc_starts),
            (0, x_quant),
            (0, scale_exp),
            (0, dt_raw),
            (0, dt_bias.reshape(1, HEADS)),
            (0, alog_row),
            (0, b_proj),
            (0, c_proj),
            (0, grad_out),
        ],
        [((TOK, 2048), BF16), ((6, HEADS, TOK), F32), ((TOK, 128), F32), ((PAIRS, 128), F32)]
        + [(part_shape, F32)] * (2 * PARTS),
        "states",
    )
    x_vals, rows, cols, kappa = made[:4]
    sends, keeps = made[4 : 4 + PARTS], made[4 + PARTS :]
    recvs = [other_core(s) for s in sends]
    chunks = []
    for part in range(PARTS):
        cut = call(
            chip_kernel,
            [(1, place), (0, keeps[part]), (0, recvs[part])],
            [(chunk_shape, F32)] * CHIPS,
            "chip_total",
        )
        chunks.append([cut[0]] + [along_z(cut[CHIPS - k], -k) for k in range(1, CHIPS)])
    within = []

    def within_slab(part, after):
        made = call(
            functools.partial(within_kernel, part),
            [
                (1, doc_starts),
                (1, skip_weight),
                (0, x_vals),
                (0, grad_out),
                (0, b_proj),
                (0, c_proj),
                (0, rows),
                (0, cols),
            ]
            + [(0, v[2]) for v in within[-1:]]
            + [(2, after)],
            [
                ((TOK, PART_PAIRS * 128), F32),
                ((2, 2 * PART_PAIRS, TOK), F32),
                ((2, TOK, 128), F32),
                ((PART_ROWS, 128), F32),
                ((PART_ROWS, 128), F32),
                ((2 * PART_PAIRS, 128), F32),
            ],
            "within",
            scratch=[pltpu.VMEM((TOK, PART_PAIRS * 128), F32)],
        )
        within.append(made)

    within_slab(0, chunks[-1][0])
    row_totals = []
    for part in range(PARTS):
        (row,) = call(
            row_kernel,
            [(1, place)] + [(0, chunks[part][k]) for k in ORDER_ROW] + [(2, within[0][1] if part == 0 else rows)],
            [(chunk_shape, F32)],
            "row_total",
        )
        row_totals.append(row)
    before = [[onward_y(row, k) for k in range(1, ROWS)] for row in row_totals]
    pieces = []
    for part in range(PARTS):
        out = call(
            entry_kernel,
            [(1, place)]
            + [(0, before[part][k]) for k in ORDER_Y]
            + [(0, chunks[part][k]) for k in ORDER_ENTRY]
            + [(2, rows)],
            [((CHUNK_ROWS, 128), F32)] * CHIPS,
            "entries",
        )
        if part == 0:
            within_slab(1, out[0])
        pieces.append([out[0]] + [along_z(out[CHIPS - k], -k) for k in range(1, CHIPS)])
    gx_parts, dt_parts, finals = [], [], []

    def final(part, sums, gx, entry, leave, after):
        ins = [x_vals, grad_out, b_proj, c_proj, rows, cols, sums, gx, alog_row, entry, leave]
        return call(
            functools.partial(final_kernel, part),
            [(0, v) for v in ins] + [(2, after)],
            [((TOK, PART_PAIRS * 128), BF16), ((2 * PART_PAIRS, TOK), F32)],
            "final",
            scratch=[pltpu.VMEM((2 * TOK + 8, PART_PAIRS * 128), F32)],
        )

    bc = within[-1][2]
    heads = None
    for part in range(PARTS):
        gx, sums, _, u, w, start = within[part]
        (mine,) = call(
            assemble_kernel,
            [(1, place)] + [(0, pieces[part][k]) for k in ORDER_ASSEMBLE] + [(2, pieces[-1][0]), (2, within[part][1])],
            [((PART_ROWS, 128), F32)],
            "assemble",
        )
        theirs = other_core(mine)
        entry, leave = call(
            functools.partial(whole_kernel, part),
            [(1, place), (0, recvs[part]), (0, mine), (0, theirs)]
            + [(2, bc)],
            [((PART_ROWS, 128), F32)] * 2,
            "whole",
        )
        (bc,) = call(
            functools.partial(sums_kernel, part),
            [(0, v) for v in [x_vals, grad_out, cols, bc, entry, leave]],
            [((2, TOK, 128), F32)],
            "sums",
        )
        (heads,) = call(
            functools.partial(logs_kernel, part),
            [(0, v) for v in [u, w, kappa, start, entry, leave]]
            + ([(0, heads)] if part else []),
            [((2 * PART_PAIRS * (part + 1), 128), F32)],
            "logs",
        )
        if part == 0:
            gx_part, dt_part = final(part, sums, gx, entry, leave, bc)
            gx_parts.append(gx_part)
            dt_parts.append(dt_part)
        else:
            finals.append((part, sums, gx, entry, leave))
    for part, sums, gx, entry, leave in finals:
        gx_part, dt_part = final(part, sums, gx, entry, leave, bc)
        gx_parts.append(gx_part)
        dt_parts.append(dt_part)
    others = [lax.ppermute(bc, "head", [(i, (i + k) % 4) for i in range(4)]) for k in (1, 2, 3)]
    (heads,) = call(
        add_kernel,
        [(0, heads), (0, other_core(heads)), (2, bc)],
        [((2 * PAIRS, 128), F32)],
        "chip_heads",
    )
    heads = heads + along_z(heads, 1) + along_z(heads, 2) + along_z(heads, 3)
    head_grads, grad_bc = call(
        heads_kernel,
        [(0, heads)] + [(0, along_y(heads, k)) for k in (1, 2, 3)] + [(0, v) for v in [bc] + others],
        [((2, HEADS), F32), ((2, TOK, 128), F32)],
        "last",
    )
    grad_x, grad_dt = call(
        join_kernel,
        [(0, v) for v in gx_parts + dt_parts] + [(2, heads)],
        [((TOK, 2048), BF16), ((HEADS, TOK), F32)],
        "join",
    )
    return (grad_x, grad_dt, grad_bc, head_grads)


def solution(mesh):
    in_specs = (
        P("seq", "head"),
        P("head", "seq"),
        P("head", "seq"),
        P("head"),
        P("head"),
        P("head"),
        P("seq", None),
        P("seq", None),
        P("seq", None),
        P("seq", "head"),
    )
    out_specs = (P("seq", "head"), P("head", "seq"), P(None, "seq", None), P(None, "head"))
    return jax.shard_map(local, mesh=mesh, in_specs=in_specs, out_specs=out_specs, check_vma=False)
```
